128 devices in a mesh: row: 8 (over x, core), col: 16 (over z, y).
Axes of the slice: x: 4, y: 4, z: 4, core: 2. Of those that a mesh axis runs over, the one named last changes fastest.
Arguments:
- right_side: float32 [2048, 288], P(('row', 'col'))
- diag_blocks: float32 [2048, 288, 288], P(('row', 'col')), as said below
- precond: float32 [2048, 288, 288], P(('row', 'col'))
- tile_values: float32 [8, 16, 32, 288, 288], P('row', 'col'), may hold values from -0.09375 to 0.09375
- pair_rows: int32 [8, 16, 32], P('row', 'col'), may hold values from 0 to 255
- pair_cols: int32 [8, 16, 32], P('row', 'col'), may hold values from 0 to 127
- tile_counts: int32 [8, 16], P('row', 'col'), may hold values from 8 to 32, as said below
Outputs:
- solution: float32 [2048, 288], P(('row', 'col'))
- residual: float32 [2048, 288], P(('row', 'col'))
The draws below stay inside these ranges and needn't reach their ends.
Inputs may be any that keep to these rules, and one draw needn't show every extreme that they name: `tile_counts`: slots at or beyond an owner's count hold indices that must be ignored; some owner holds exactly 32 live slots. `diag_blocks`: every diagonal block and every preconditioner block is symmetric positive definite.
All inputs are finite; a program needn't handle non-finite values.
Results may differ from the reference program's by a relative error of at most 0.0004.
Values sent between devices are 32-bit elements; how exact they have to be, the bound alone decides.
A program may use at most 128 MiB of HBM per device.

```python
import jax
import jax.numpy as jnp
from jax import lax

B = 288
TD = 16
SLOTS = 32
ITERS = 3
GRID_ROWS = 8
GRID_COLS = 16
NT = 2048
RT = 256
CT = 128


def diagonal_parts(key):
    key_diag, key_noise = jax.random.split(key)
    diag_vals = jax.random.uniform(key_diag, (NT, B), jnp.float32, 3.0, 6.0)
    noise = jax.random.normal(key_noise, (NT, B, B), jnp.float32) * (0.5 / 17.0)
    sym_noise = 0.5 * (noise + jnp.swapaxes(noise, 1, 2))
    ident = (jnp.arange(B)[:, None] == jnp.arange(B)[None, :]).astype(jnp.float32)
    off_part = sym_noise * (1.0 - ident)[None]
    return (diag_vals, off_part, ident)


def draw_diag_blocks(key, part):
    diag_vals, off_part, ident = diagonal_parts(key)
    return diag_vals[:, :, None] * ident[None] + off_part


def draw_precond(key, part):
    diag_vals, off_part, ident = diagonal_parts(key)
    inverse_diag = 1.0 / diag_vals
    return inverse_diag[:, :, None] * ident[None] - off_part * inverse_diag[:, :, None] * inverse_diag[:, None, :]


def draw_right_side(key, part):
    key = jax.random.fold_in(key, 13)
    key_scale, key_vals = jax.random.split(key)
    tile_pos = jnp.arange(NT, dtype=jnp.float32)[:, None]
    ramp = 1.0 + 2.0 * tile_pos / max(NT - 1, 1)
    row_scale = 0.3 * 10.0 ** jax.random.uniform(key_scale, (NT, 1), jnp.float32)
    values = jax.random.normal(key_vals, (NT, B), jnp.float32)
    return values * row_scale * ramp


def draw_tile_counts(key, part):
    key = jax.random.fold_in(key, 14)
    key_counts, key_pick = jax.random.split(key)
    counts = jax.random.randint(key_counts, (GRID_ROWS * GRID_COLS,), max(1, SLOTS // 4), SLOTS + 1)
    pick = jax.random.randint(key_pick, (), 0, GRID_ROWS * GRID_COLS)
    counts = jnp.where(jnp.arange(GRID_ROWS * GRID_COLS) == pick, SLOTS, counts)
    return counts.reshape(GRID_ROWS, GRID_COLS).astype(jnp.int32)


def with_ends(values, own_key, least, top_value):
    longest = values.shape.index(max(values.shape))
    spots = []
    for shift in (0, 1):
        where = [jax.random.randint(jax.random.fold_in(own_key, axis), (), 0, length) for axis, length in enumerate(values.shape)]
        where[longest] = (where[longest] + shift) % values.shape[longest]
        spots.append(tuple(where))
    return values.at[spots[0]].set(least).at[spots[1]].set(top_value)


def steps_of(key, dims, cuts, smallest, high):
    gain, own = 1.0, jax.random.fold_in(key, 6)
    for dim, parts in cuts:
        heights = jnp.exp(jax.random.uniform(jax.random.fold_in(own, dim), (parts,), jnp.float32, smallest / len(cuts), high / len(cuts)))
        gain = gain * jnp.repeat(heights, dims[dim] // parts).reshape([-1 if axis == dim else 1 for axis in range(len(dims))])
    return gain


def scatter_about(key, shape, scale, reach, shards=(), kind=jnp.bfloat16):
    values = scale * jax.random.normal(key, shape, jnp.float32)
    if shards:
        values = values * steps_of(key, shape, shards, -0.22, 0.18)
    return jnp.clip(values, -reach, reach).astype(kind)


def setup_inputs(seed: int = 0) -> dict:
    key_of = jax.random.split(jax.random.key(seed), 8)
    right_side = draw_right_side(jax.random.fold_in(key_of[7], 71), 0)
    diag_blocks = draw_diag_blocks(jax.random.fold_in(key_of[7], 71), 0)
    precond = draw_precond(jax.random.fold_in(key_of[7], 71), 0)
    tile_values = scatter_about(key_of[3], (GRID_ROWS, GRID_COLS, SLOTS, B, B), (0.1 / 17), 0.09375, ((0, 8), (1, 16)), jnp.float32)
    pair_rows = with_ends(jax.random.randint(key_of[4], (GRID_ROWS, GRID_COLS, SLOTS), 0, RT), jax.random.fold_in(key_of[4], 1), 0, RT - 1).astype(jnp.int32)
    pair_cols = with_ends(jax.random.randint(key_of[5], (GRID_ROWS, GRID_COLS, SLOTS), 0, CT), jax.random.fold_in(key_of[5], 1), 0, CT - 1).astype(jnp.int32)
    tile_counts = draw_tile_counts(jax.random.fold_in(key_of[7], 71), 0)
    return {"right_side": right_side, "diag_blocks": diag_blocks, "precond": precond, "tile_values": tile_values, "pair_rows": pair_rows, "pair_cols": pair_cols, "tile_counts": tile_counts}


def schur_product(vec, diag_blocks, tile_values, glob_rows, glob_cols, live):
    hp = lax.Precision.HIGHEST
    local = jnp.einsum('tab,tb->ta', diag_blocks, vec, precision=hp)
    fwd = jnp.einsum('rcsab,rcsb->rcsa', tile_values, vec[glob_cols], precision=hp) * live[..., None]
    back = jnp.einsum('rcsab,rcsa->rcsb', tile_values, vec[glob_rows], precision=hp) * live[..., None]
    width = vec.shape[1]
    added = jax.ops.segment_sum(fwd.reshape(-1, width), glob_rows.reshape(-1), num_segments=NT)
    added = added + jax.ops.segment_sum(back.reshape(-1, width), glob_cols.reshape(-1), num_segments=NT)
    return local + added


def reference(right_side, diag_blocks, precond, tile_values, pair_rows, pair_cols, tile_counts):
    hp = lax.Precision.HIGHEST
    grid_r = jnp.arange(GRID_ROWS, dtype=jnp.int32)[:, None, None]
    grid_c = jnp.arange(GRID_COLS, dtype=jnp.int32)[None, :, None]
    glob_rows = (grid_r * RT + pair_rows).astype(jnp.int32)
    glob_cols = ((pair_cols // TD) * RT + grid_c * TD + pair_cols % TD).astype(jnp.int32)
    slot_ids = jnp.arange(SLOTS, dtype=jnp.int32)[None, None, :]
    live = (slot_ids < tile_counts[:, :, None]).astype(jnp.float32)
    solution = jnp.zeros_like(right_side)
    residual = right_side
    precon_r = jnp.einsum('tab,tb->ta', precond, residual, precision=hp)
    direction = precon_r
    rz_now = jnp.sum(residual * precon_r)
    for step in range(ITERS):
        image = schur_product(direction, diag_blocks, tile_values, glob_rows, glob_cols, live)
        alpha = rz_now / jnp.sum(direction * image)
        solution = solution + alpha * direction
        residual = residual - alpha * image
        if step + 1 < ITERS:
            precon_r = jnp.einsum('tab,tb->ta', precond, residual, precision=hp)
            rz_next = jnp.sum(residual * precon_r)
            direction = precon_r + (rz_next / rz_now) * direction
            rz_now = rz_next
    return solution, residual
```

```python
import functools

import jax
import jax.numpy as jnp
from jax import lax
from jax.experimental import pallas as pl
from jax.experimental.pallas import tpu as pltpu
from jax.sharding import PartitionSpec as P

ITERS = 3
LANES = 128
MESH = pl.DeviceIdType.MESH
F32 = jnp.float32
BF16 = jnp.bfloat16


def three_parts(value):
    high = value.astype(BF16)
    rest = value - high.astype(F32)
    middle = rest.astype(BF16)
    low = (rest - middle.astype(F32)).astype(BF16)
    return high, middle, low


def apply_blocks(blocks, vec, out, first, last):
    width = blocks.shape[1]
    turned = jnp.transpose(vec)
    for t in range(first, last):
        out[t : t + 1, 0:width] = jnp.sum(blocks[t] * turned[0:width, t : t + 1], axis=0, keepdims=True)


def total(value):
    return jnp.sum(jnp.sum(value, axis=0, keepdims=True), axis=1, keepdims=True)


def kernel(
    n_row, n_col,
    rows_s, cols_s, count_s, rows_v, cols_v, rhs, diag_hbm, prec_hbm, tile_hbm,
    sol_out, res_out,
    tiles, diag, prec,
    msg, got_row0, got_row1, got_row2, got_col0, got_col1, got_col2, sum_row, sum_col, out_row, out_col,
    picked, backs, local, stage, dots, dot_col, dot_row,
    x_v, r_v, p_v, s_v,
    prec_sem, diag_sem, tile_sem,
    msg_col_ssem, msg_row_ssem, got_row_sem, got_col_sem,
    out_row_ssem, out_col_ssem, sum_row_sem, sum_col_sem,
    dot_ssem, dot_rsem,
):
    got_row_of, got_col_of = (got_row0, got_row1, got_row2), (got_col0, got_col1, got_col2)
    per_dev, width = rhs.shape
    slots = tiles.shape[0]
    wide = msg.shape[2]
    spare = wide - LANES
    first_lane = width - spare
    my_row = lax.axis_index("row")
    my_col = lax.axis_index("col")

    part = per_dev // 4
    for k in range(4):
        pltpu.make_async_copy(
            prec_hbm.at[pl.ds(k * part, part)], prec.at[pl.ds(k * part, part)], prec_sem.at[k]
        ).start()
    pltpu.make_async_copy(diag_hbm, diag, diag_sem).start()
    pltpu.make_async_copy(tile_hbm, tiles, tile_sem).start()

    barrier = pltpu.get_barrier_semaphore()

    def greet_col(i, _):
        pl.semaphore_signal(barrier, inc=1, device_id=(my_row, lax.rem(my_col + i, n_col)), device_id_type=MESH)
        return 0

    def greet_row(i, _):
        pl.semaphore_signal(barrier, inc=1, device_id=(lax.rem(my_row + i, n_row), my_col), device_id_type=MESH)
        return 0

    lax.fori_loop(1, n_col, greet_col, 0)
    lax.fori_loop(1, n_row, greet_row, 0)

    def to_cols(source, target, send_sem, recv_sem):
        def step(i, _):
            peer = lax.rem(my_col + i, n_col)
            pltpu.make_async_remote_copy(
                src_ref=source(peer), dst_ref=target, send_sem=send_sem, recv_sem=recv_sem,
                device_id=(my_row, peer), device_id_type=MESH,
            ).start()
            return 0
        lax.fori_loop(1, n_col, step, 0)

    def to_rows(source, target, send_sem, recv_sem):
        def step(i, _):
            peer = lax.rem(my_row + i, n_row)
            pltpu.make_async_remote_copy(
                src_ref=source(peer), dst_ref=target, send_sem=send_sem, recv_sem=recv_sem,
                device_id=(peer, my_col), device_id_type=MESH,
            ).start()
            return 0
        lax.fori_loop(1, n_row, step, 0)

    def wait_bytes(ref, sem):
        pltpu.make_async_copy(ref, ref, sem).wait()

    def block(index):
        return pl.ds(pl.multiple_of(index * per_dev, per_dev), per_dev)

    col_blocks = pl.ds(0, (n_col - 1) * per_dev)
    row_blocks = pl.ds(0, (n_row - 1) * per_dev)

    count = count_s[0, 0]
    slot_lane = lax.broadcasted_iota(jnp.int32, (n_col * per_dev, slots), 1)
    tile_of = lax.broadcasted_iota(jnp.int32, (n_col * per_dev, slots), 0)
    pick_row = ((tile_of == rows_v[...]) & (slot_lane < count)).astype(F32)
    pick_row = jnp.concatenate([pick_row, jnp.zeros((n_col * per_dev, LANES - slots), F32)], axis=1).astype(BF16)
    pick_row = jnp.concatenate([pick_row] * 3, axis=1)
    slot_lane = lax.broadcasted_iota(jnp.int32, (n_row * per_dev, slots), 1)
    tile_of = lax.broadcasted_iota(jnp.int32, (n_row * per_dev, slots), 0)
    pick_col = ((tile_of == cols_v[...]) & (slot_lane < count)).astype(F32)
    pick_col = jnp.concatenate([pick_col] * 3, axis=1).astype(BF16)

    lane = lax.broadcasted_iota(jnp.int32, (per_dev, wide), 1)
    sub = lax.broadcasted_iota(jnp.int32, (per_dev, wide), 0)
    valid = lane < width

    head = lax.broadcasted_iota(jnp.int32, (n_col * per_dev, LANES), 0) % per_dev == 0
    dot_lane = lax.broadcasted_iota(jnp.int32, (8, LANES), 1)

    for ref in (local, stage, backs, x_v, r_v):
        ref[...] = jnp.zeros_like(ref)
    r_v[:, 0:width] = rhs[...]

    residual = r_v[...]
    for k in range(4):
        pltpu.make_async_copy(
            prec_hbm.at[pl.ds(k * part, part)], prec.at[pl.ds(k * part, part)], prec_sem.at[k]
        ).wait()
        apply_blocks(prec, residual, stage, k * part, (k + 1) * part)
    z = stage[...]
    msg[0] = z + jnp.where((sub == 0) & (lane == width), total(residual * z), 0.0)

    pl.semaphore_wait(barrier, n_col + n_row - 2)

    for j in range(ITERS):
        got_row, got_col = got_row_of[j], got_col_of[j]
        to_rows(lambda peer: msg.at[j], got_col.at[block(my_row)], msg_row_ssem.at[j], got_col_sem.at[j])
        to_cols(lambda peer: msg.at[j], got_row.at[block(my_col)], msg_col_ssem.at[j], got_row_sem.at[j])
        vec = msg[j]
        got_col[block(my_row), :] = vec
        got_row[block(my_col), :] = vec
        z = jnp.where(valid, vec, 0.0)

        if j == 0:
            pltpu.make_async_copy(diag_hbm, diag, diag_sem).wait()
        apply_blocks(diag, vec, local, 0, per_dev)
        delta = total(z * local[...])

        if j == 0:
            pltpu.make_async_copy(tile_hbm, tiles, tile_sem).wait()
        wait_bytes(got_col.at[row_blocks], got_col_sem.at[j])
        turned_lane = lax.broadcasted_iota(jnp.int32, (width, LANES), 1)
        products = jnp.zeros((width, LANES), F32)
        for slot in range(slots):
            index = jnp.clip(cols_s[0, slot], 0, n_row * per_dev - 1)
            product = jnp.sum(tiles[slot] * got_col[pl.ds(index, 1), 0:width], axis=1, keepdims=True)
            products = jnp.where(turned_lane == slot, product, products)
        products = jnp.where(turned_lane < count, products, 0.0)
        filled = jnp.concatenate([products, jnp.zeros((wide - width, LANES), F32)], axis=0)
        out_row[j] = lax.dot_general(
            pick_row, jnp.concatenate(three_parts(filled), axis=1),
            (((1,), (1,)), ((), ())), preferred_element_type=F32,
        )
        to_cols(lambda peer: out_row.at[j, block(peer)], sum_row.at[j, block(my_col)], out_row_ssem.at[j], sum_row_sem.at[j])
        sum_row[j, block(my_col), :] = out_row[j, block(my_col), :]

        wait_bytes(got_row.at[col_blocks], got_row_sem.at[j])
        for slot in range(slots):
            index = jnp.clip(rows_s[0, slot], 0, n_col * per_dev - 1)
            picked[slot : slot + 1, :] = got_row[pl.ds(index, 1), :]
        turned = jnp.transpose(picked[...])
        delta = delta + 2.0 * total(products[:, 0:slots] * turned[0:width, :])
        partial = jnp.sum(jnp.where(head, got_row[:, spare:wide], 0.0), axis=0, keepdims=True)
        dots[j, 0] = jnp.where(dot_lane == 0, delta, jnp.where(dot_lane >= first_lane, partial, 0.0))
        to_rows(lambda peer: dots.at[j, 0], dot_col.at[j, my_row], dot_ssem.at[j, 0], dot_rsem.at[j, 0])
        dot_col[j, my_row] = dots[j, 0]

        for slot in range(slots):
            backs[slot : slot + 1, 0:width] = jnp.sum(
                tiles[slot] * turned[0:width, slot : slot + 1], axis=0, keepdims=True
            )
        live = lax.broadcasted_iota(jnp.int32, (slots, wide), 0) < count
        out_col[j] = jnp.dot(
            pick_col, jnp.concatenate(three_parts(jnp.where(live, backs[...], 0.0)), axis=0),
            preferred_element_type=F32,
        )
        to_rows(lambda peer: out_col.at[j, block(peer)], sum_col.at[j, block(my_row)], out_col_ssem.at[j], sum_col_sem.at[j])
        sum_col[j, block(my_row), :] = out_col[j, block(my_row), :]

        wait_bytes(dot_col.at[j, pl.ds(0, n_row - 1)], dot_rsem.at[j, 0])
        sums = jnp.sum(dot_col[j], axis=0)
        dots[j, 1] = sums
        to_cols(lambda peer: dots.at[j, 1], dot_row.at[j, my_col], dot_ssem.at[j, 1], dot_rsem.at[j, 1])
        dot_row[j, my_col] = sums
        gamma = sums[0:1, first_lane : first_lane + 1]
        cross = sums[0:1, first_lane + 1 : first_lane + 2]

        wait_bytes(sum_col.at[j, row_blocks], sum_col_sem.at[j])
        image = local[...]
        for k in range(n_row):
            image = image + sum_col[j, k * per_dev : (k + 1) * per_dev, :]
        wait_bytes(sum_row.at[j, col_blocks], sum_row_sem.at[j])
        for k in range(n_col):
            image = image + sum_row[j, k * per_dev : (k + 1) * per_dev, :]

        wait_bytes(dot_row.at[j, pl.ds(0, n_col - 1)], dot_rsem.at[j, 1])
        curve = jnp.sum(dot_row[j], axis=0)[0:1, 0:1]
        if j > 0:
            beta = gamma / old_gamma
            curve = curve + beta * (cross + beta * old_curve)
            z = z + beta * p_v[...]
            image = image + beta * s_v[...]
        alpha = gamma / curve
        old_gamma, old_curve = gamma, curve
        x_v[...] = x_v[...] + alpha * z
        r_v[...] = r_v[...] - alpha * image

        if j < ITERS - 1:
            p_v[...] = z
            s_v[...] = image
            residual = r_v[...]
            apply_blocks(prec, residual, stage, 0, per_dev)
            z = stage[...]
            aside = jnp.where(lane == width, total(residual * z), 2.0 * total(z * image))
            msg[j + 1] = z + jnp.where((sub == 0) & (lane >= width) & (lane < width + 2), aside, 0.0)

    sol_out[...] = x_v[:, 0:width]
    res_out[...] = r_v[:, 0:width]

    for j in range(ITERS):
        wait_bytes(got_col_of[j].at[row_blocks], msg_row_ssem.at[j])
        wait_bytes(got_row_of[j].at[col_blocks], msg_col_ssem.at[j])
        wait_bytes(sum_row.at[j, col_blocks], out_row_ssem.at[j])
        wait_bytes(sum_col.at[j, row_blocks], out_col_ssem.at[j])
        wait_bytes(dot_col.at[j, pl.ds(0, n_row - 1)], dot_ssem.at[j, 0])
        wait_bytes(dot_row.at[j, pl.ds(0, n_col - 1)], dot_ssem.at[j, 1])


def per_device(right_side, diag_blocks, precond, tile_values, pair_rows, pair_cols, tile_counts):
    n_row = lax.axis_size("row")
    n_col = lax.axis_size("col")
    per_dev, width = right_side.shape
    slots = tile_values.shape[2]
    wide = -(-(width + 2) // LANES) * LANES
    rows_here = pair_rows[0]
    cols_here = pair_cols[0]
    smem = pl.BlockSpec(memory_space=pltpu.SMEM)
    vmem = pl.BlockSpec(memory_space=pltpu.VMEM)
    anywhere = pl.BlockSpec(memory_space=pl.ANY)
    vector = pltpu.VMEM((per_dev, wide), F32)
    row_area = pltpu.VMEM((ITERS, n_col * per_dev, wide), F32)
    col_area = pltpu.VMEM((ITERS, n_row * per_dev, wide), F32)
    got_rows = [pltpu.VMEM((n_col * per_dev, wide), F32)] * ITERS
    got_cols = [pltpu.VMEM((n_row * per_dev, wide), F32)] * ITERS
    each = pltpu.SemaphoreType.DMA((ITERS,))
    return pl.pallas_call(
        functools.partial(kernel, n_row, n_col),
        out_shape=(jax.ShapeDtypeStruct((per_dev, width), F32),) * 2,
        in_specs=[smem, smem, smem, vmem, vmem, vmem, anywhere, anywhere, anywhere],
        out_specs=(vmem, vmem),
        scratch_shapes=[
            pltpu.VMEM((slots, width, width), F32),
            pltpu.VMEM((per_dev, width, width), F32),
            pltpu.VMEM((per_dev, width, width), F32),
            pltpu.VMEM((ITERS, per_dev, wide), F32),
            *got_rows, *got_cols, row_area, col_area, row_area, col_area,
            pltpu.VMEM((slots, wide), F32),
            pltpu.VMEM((slots, wide), F32),
            vector, vector,
            pltpu.VMEM((ITERS, 2, 8, LANES), F32),
            pltpu.VMEM((ITERS, n_row, 8, LANES), F32),
            pltpu.VMEM((ITERS, n_col, 8, LANES), F32),
            vector, vector, vector, vector,
            pltpu.SemaphoreType.DMA((4,)),
            pltpu.SemaphoreType.DMA,
            pltpu.SemaphoreType.DMA,
            each, each, each, each, each, each, each, each,
            pltpu.SemaphoreType.DMA((ITERS, 2)),
            pltpu.SemaphoreType.DMA((ITERS, 2)),
        ],
        compiler_params=pltpu.CompilerParams(
            collective_id=0, has_side_effects=True, vmem_limit_bytes=56 * 2**20
        ),
    )(
        rows_here, cols_here, tile_counts, rows_here, cols_here,
        right_side, diag_blocks, precond, tile_values[0, 0],
    )


def solution(mesh):
    return jax.shard_map(
        per_device,
        mesh=mesh,
        in_specs=(
            P(("row", "col"), None),
            P(("row", "col"), None, None),
            P(("row", "col"), None, None),
            P("row", "col", None, None, None),
            P("row", "col", None),
            P("row", "col", None),
            P("row", "col"),
        ),
        out_specs=(P(("row", "col"), None), P(("row", "col"), None)),
        check_vma=False,
    )
```

```python
import functools

import jax
import jax.numpy as jnp
from jax import lax
from jax.experimental import pallas as pl
from jax.experimental.pallas import tpu as pltpu
from jax.sharding import PartitionSpec as P

ITERS = 3
LANES = 128
MESH = pl.DeviceIdType.MESH
F32 = jnp.float32
BF16 = jnp.bfloat16


def three_parts(value):
    high = value.astype(BF16)
    rest = value - high.astype(F32)
    middle = rest.astype(BF16)
    low = (rest - middle.astype(F32)).astype(BF16)
    return high, middle, low


def apply_blocks(blocks, vec, out, first, last):
    width = blocks.shape[1]
    turned = jnp.transpose(vec)
    for t in range(first, last):
        out[t : t + 1, 0:width] = jnp.sum(blocks[t] * turned[0:width, t : t + 1], axis=0, keepdims=True)


def total(value):
    return jnp.sum(jnp.sum(value, axis=0, keepdims=True), axis=1, keepdims=True)


def kernel(
    n_row, n_col,
    rows_s, cols_s, count_s, rows_v, cols_v, rhs, diag_hbm, prec_hbm, tile_hbm,
    both_out,
    tiles, diag, prec,
    msg, got_row0, got_row1, got_row2, got_col0, got_col1, got_col2, sum_row, sum_col, out_row, out_col,
    picked, backs, local, dots, dot_col, dot_row,
    x_v, rh_v, z_v, w_v, r_v, s_v, p_v,
    prec_sem, diag_sem, tile_sem,
    msg_col_ssem, msg_row_ssem, got_row_sem, got_col_sem,
    out_row_ssem, out_col_ssem, sum_row_sem, sum_col_sem,
    dot_ssem, dot_rsem,
):
    got_row_of, got_col_of = (got_row0, got_row1, got_row2), (got_col0, got_col1, got_col2)
    per_dev, width = rhs.shape
    slots = tiles.shape[0]
    wide = msg.shape[2]
    my_row = lax.axis_index("row")
    my_col = lax.axis_index("col")

    part = per_dev // 4
    for k in range(4):
        pltpu.make_async_copy(
            prec_hbm.at[pl.ds(k * part, part)], prec.at[pl.ds(k * part, part)], prec_sem.at[k]
        ).start()
    pltpu.make_async_copy(diag_hbm, diag, diag_sem).start()
    pltpu.make_async_copy(tile_hbm, tiles, tile_sem).start()

    barrier = pltpu.get_barrier_semaphore()

    side = 4
    my_z, my_y = my_col // side, my_col % side
    my_x, my_core = my_row // 2, my_row % 2
    far = (2, 1, 3, 0)
    col_peers = [
        lax.rem(my_z + dz, side) * side + lax.rem(my_y + dy, side)
        for dz, dy in sorted(
            ((dz, dy) for dz in far for dy in far if dz or dy),
            key=lambda d: -(min(d[0], side - d[0]) + min(d[1], side - d[1])),
        )
    ]
    row_peers = [
        lax.rem(my_x + dx, side) * 2 + lax.rem(my_core + dc, 2)
        for dx in far for dc in (0, 1) if dx or dc
    ]

    for peer in col_peers:
        pl.semaphore_signal(barrier, inc=1, device_id=(my_row, peer), device_id_type=MESH)
    for peer in row_peers:
        pl.semaphore_signal(barrier, inc=1, device_id=(peer, my_col), device_id_type=MESH)

    def to_cols(source, target, send_sem, recv_sem):
        for peer in col_peers:
            pltpu.make_async_remote_copy(
                src_ref=source(peer), dst_ref=target, send_sem=send_sem, recv_sem=recv_sem,
                device_id=(my_row, peer), device_id_type=MESH,
            ).start()

    def to_rows(source, target, send_sem, recv_sem):
        for peer in row_peers:
            pltpu.make_async_remote_copy(
                src_ref=source(peer), dst_ref=target, send_sem=send_sem, recv_sem=recv_sem,
                device_id=(peer, my_col), device_id_type=MESH,
            ).start()

    def wait_bytes(ref, sem):
        pltpu.make_async_copy(ref, ref, sem).wait()

    def block(index):
        return pl.ds(pl.multiple_of(index * per_dev, per_dev), per_dev)

    col_blocks = pl.ds(0, (n_col - 1) * per_dev)
    row_blocks = pl.ds(0, (n_row - 1) * per_dev)

    count = count_s[0, 0]
    slot_lane = lax.broadcasted_iota(jnp.int32, (n_col * per_dev, slots), 1)
    tile_of = lax.broadcasted_iota(jnp.int32, (n_col * per_dev, slots), 0)
    pick_row = ((tile_of == rows_v[...]) & (slot_lane < count)).astype(F32)
    pick_row = jnp.concatenate([pick_row, jnp.zeros((n_col * per_dev, LANES - slots), F32)], axis=1).astype(BF16)
    pick_row = jnp.concatenate([pick_row] * 3, axis=1)
    slot_lane = lax.broadcasted_iota(jnp.int32, (n_row * per_dev, slots), 1)
    tile_of = lax.broadcasted_iota(jnp.int32, (n_row * per_dev, slots), 0)
    pick_col = ((tile_of == cols_v[...]) & (slot_lane < count)).astype(F32)
    pick_col = jnp.concatenate([pick_col] * 3, axis=1).astype(BF16)

    dot_lane = lax.broadcasted_iota(jnp.int32, (8, LANES), 1)

    for ref in (local, backs, x_v, rh_v, msg):
        ref[...] = jnp.zeros_like(ref)
    rh_v[:, 0:width] = rhs[...]

    residual = rh_v[...]
    for k in range(4):
        pltpu.make_async_copy(
            prec_hbm.at[pl.ds(k * part, part)], prec.at[pl.ds(k * part, part)], prec_sem.at[k]
        ).wait()
        apply_blocks(prec, residual, msg.at[0], k * part, (k + 1) * part)

    pl.semaphore_wait(barrier, n_col + n_row - 2)

    def small(j, k, along_row):
        if along_row:
            target, me, send = dot_row.at[j, k], my_col, to_cols
        else:
            target, me, send = dot_col.at[j, k], my_row, to_rows
        send(lambda peer: dots.at[j, k], target.at[me], dot_ssem.at[j, k], dot_rsem.at[j, k])
        target[me] = dots[j, k]

    def small_sum(j, k, along_row):
        source, peers = (dot_row, n_col - 1) if along_row else (dot_col, n_row - 1)
        wait_bytes(source.at[j, k, pl.ds(0, peers)], dot_rsem.at[j, k])
        return jnp.sum(source[j, k], axis=0)

    def in_lanes(*values):
        packed = jnp.zeros((8, LANES), F32)
        for k, value in enumerate(values):
            packed = jnp.where(dot_lane == k, value, packed)
        return packed

    def lanes_of(packed, n):
        return [packed[0:1, k : k + 1] for k in range(n)]

    for j in range(ITERS):
        last = j == ITERS - 1
        got_row, got_col = got_row_of[j], got_col_of[j]
        to_rows(lambda peer: msg.at[j], got_col.at[block(my_row)], msg_row_ssem.at[j], got_col_sem.at[j])
        to_cols(lambda peer: msg.at[j], got_row.at[block(my_col)], msg_col_ssem.at[j], got_row_sem.at[j])
        zh = msg[j]
        rh = rh_v[...]
        got_col[block(my_row), :] = zh
        got_row[block(my_col), :] = zh

        if j == 0:
            pltpu.make_async_copy(diag_hbm, diag, diag_sem).wait()
        apply_blocks(diag, zh, local, 0, per_dev)
        own = zh * local[...]
        early = [total(own), total(rh * zh)]
        if j > 0:
            z, w, r, s = z_v[...], w_v[...], r_v[...], s_v[...]
            early += [total(rh * z + r * zh), total(zh * w), total(zh * s), total(z * s)]
        dots[j, 0] = in_lanes(*early)
        small(j, 0, True)

        if j == 0:
            pltpu.make_async_copy(tile_hbm, tiles, tile_sem).wait()
        wait_bytes(got_col.at[row_blocks], got_col_sem.at[j])
        turned_lane = lax.broadcasted_iota(jnp.int32, (width, LANES), 1)
        products = jnp.zeros((width, LANES), F32)
        for slot in range(slots):
            index = jnp.clip(cols_s[0, slot], 0, n_row * per_dev - 1)
            product = jnp.sum(tiles[slot] * got_col[pl.ds(index, 1), 0:width], axis=1, keepdims=True)
            products = jnp.where(turned_lane == slot, product, products)
        products = jnp.where(turned_lane < count, products, 0.0)
        products = jnp.concatenate([products, jnp.zeros((wide - width, LANES), F32)], axis=0)
        products = lax.dot_general(
            pick_row, jnp.concatenate(three_parts(products), axis=1),
            (((1,), (1,)), ((), ())), preferred_element_type=F32,
        )
        out_row[j] = products

        def send_out_row():
            to_cols(lambda peer: out_row.at[j, block(peer)], sum_row.at[j, block(my_col)], out_row_ssem.at[j], sum_row_sem.at[j])
            sum_row[j, block(my_col), :] = out_row[j, block(my_col), :]

        if not last:
            send_out_row()

        wait_bytes(got_row.at[col_blocks], got_row_sem.at[j])
        shared = jnp.sum((out_row[j] * got_row[...]).reshape(n_col, per_dev, wide), axis=0)
        dots[j, 2] = in_lanes(total(own + 2.0 * shared))
        small(j, 2, last)
        if last:
            send_out_row()
        dots[j, 1] = small_sum(j, 0, True)
        small(j, 1, False)

        for slot in range(slots):
            index = jnp.clip(rows_s[0, slot], 0, n_col * per_dev - 1)
            picked[slot : slot + 1, :] = got_row[pl.ds(index, 1), :]
        turned = jnp.transpose(picked[...])
        for slot in range(slots):
            backs[slot : slot + 1, 0:width] = jnp.sum(
                tiles[slot] * turned[0:width, slot : slot + 1], axis=0, keepdims=True
            )
        live = lax.broadcasted_iota(jnp.int32, (slots, wide), 0) < count
        out_col[j] = jnp.dot(
            pick_col, jnp.concatenate(three_parts(jnp.where(live, backs[...], 0.0)), axis=0),
            preferred_element_type=F32,
        )
        to_rows(lambda peer: out_col.at[j, block(peer)], sum_col.at[j, block(my_row)], out_col_ssem.at[j], sum_col_sem.at[j])
        sum_col[j, block(my_row), :] = out_col[j, block(my_row), :]

        dots[j, 3] = small_sum(j, 2, last)
        small(j, 3, not last)

        if j == 0:
            curve_h, gamma = lanes_of(small_sum(j, 1, False), 2)
            predicted = gamma / curve_h
            z, r = zh, rh
            p = z
        else:
            curve_h, gamma_h, gamma_x, zh_w, zh_s, z_s = lanes_of(small_sum(j, 1, False), 6)
            delta_h = lanes_of(small_sum(j - 1, 3, True), 1)[0]
            if j == 1:
                delta = curve = delta_h
            else:
                delta = rest * (rest * delta_h + twice) + theta * theta * delta
                curve = delta + beta * (cross + beta * curve)
            alpha = gamma / curve
            theta = (predicted - alpha) / predicted
            rest = 1.0 - theta
            beta = (rest * (rest * gamma_h + theta * gamma_x) + theta * theta * gamma) / gamma
            gamma = beta * gamma
            cross = 2.0 * (rest * zh_s + theta * z_s)
            twice = 2.0 * theta * zh_w
            predicted = gamma_h / curve_h
            x_v[...] = x_v[...] + alpha * p_v[...]
            z = rest * zh + theta * z
            r = rest * rh + theta * r
            p = z + beta * p_v[...]
            kept_w = theta * w
            kept_s = beta * s

        wait_bytes(sum_col.at[j, row_blocks], sum_col_sem.at[j])
        image = local[...]
        for k in range(n_row):
            image = image + sum_col[j, k * per_dev : (k + 1) * per_dev, :]
        wait_bytes(sum_row.at[j, col_blocks], sum_row_sem.at[j])
        for k in range(n_col):
            image = image + sum_row[j, k * per_dev : (k + 1) * per_dev, :]
        w = image if j == 0 else rest * image + kept_w
        s = w if j == 0 else w + kept_s
        if not last:
            rh = r - predicted * s
            rh_v[...] = rh
            apply_blocks(prec, rh, msg.at[j + 1], 0, per_dev)
            z_v[...], w_v[...], r_v[...], s_v[...], p_v[...] = z, w, r, s, p

    delta_h = lanes_of(small_sum(ITERS - 1, 3, False), 1)[0]
    delta = rest * (rest * delta_h + twice) + theta * theta * delta
    alpha = gamma / (delta + beta * (cross + beta * curve))
    x = x_v[...] + alpha * p
    r = r - alpha * s
    both_out[0] = x[:, 0:width]
    both_out[1] = r[:, 0:width]

    for j in range(ITERS):
        wait_bytes(got_col_of[j].at[row_blocks], msg_row_ssem.at[j])
        wait_bytes(got_row_of[j].at[col_blocks], msg_col_ssem.at[j])
        wait_bytes(sum_row.at[j, col_blocks], out_row_ssem.at[j])
        wait_bytes(sum_col.at[j, row_blocks], out_col_ssem.at[j])
        for k in range(4):
            along_row = k == 0 or (k == 2) == (j == ITERS - 1) and k > 1
            source, peers = (dot_row, n_col - 1) if along_row else (dot_col, n_row - 1)
            wait_bytes(source.at[j, k, pl.ds(0, peers)], dot_ssem.at[j, k])


def part_kernel(both, sol_out, res_out):
    sol_out[...] = both[0]
    res_out[...] = both[1]


def per_device(right_side, diag_blocks, precond, tile_values, pair_rows, pair_cols, tile_counts):
    n_row = lax.axis_size("row")
    n_col = lax.axis_size("col")
    per_dev, width = right_side.shape
    slots = tile_values.shape[2]
    wide = -(-width // LANES) * LANES
    rows_here = pair_rows[0]
    cols_here = pair_cols[0]
    smem = pl.BlockSpec(memory_space=pltpu.SMEM)
    vmem = pl.BlockSpec(memory_space=pltpu.VMEM)
    anywhere = pl.BlockSpec(memory_space=pl.ANY)
    vector = pltpu.VMEM((per_dev, wide), F32)
    row_area = pltpu.VMEM((ITERS, n_col * per_dev, wide), F32)
    col_area = pltpu.VMEM((ITERS, n_row * per_dev, wide), F32)
    got_rows = [pltpu.VMEM((n_col * per_dev, wide), F32)] * ITERS
    got_cols = [pltpu.VMEM((n_row * per_dev, wide), F32)] * ITERS
    each = pltpu.SemaphoreType.DMA((ITERS,))
    both = pl.pallas_call(
        functools.partial(kernel, n_row, n_col),
        out_shape=jax.ShapeDtypeStruct((2, per_dev, width), F32),
        in_specs=[smem, smem, smem, vmem, vmem, vmem, anywhere, anywhere, anywhere],
        out_specs=vmem,
        scratch_shapes=[
            pltpu.VMEM((slots, width, width), F32),
            pltpu.VMEM((per_dev, width, width), F32),
            pltpu.VMEM((per_dev, width, width), F32),
            pltpu.VMEM((ITERS, per_dev, wide), F32),
            *got_rows, *got_cols, row_area, col_area, row_area, col_area,
            pltpu.VMEM((slots, wide), F32),
            pltpu.VMEM((slots, wide), F32),
            vector,
            pltpu.VMEM((ITERS, 4, 8, LANES), F32),
            pltpu.VMEM((ITERS, 4, n_row, 8, LANES), F32),
            pltpu.VMEM((ITERS, 4, n_col, 8, LANES), F32),
            vector, vector, vector, vector, vector, vector, vector,
            pltpu.SemaphoreType.DMA((4,)),
            pltpu.SemaphoreType.DMA,
            pltpu.SemaphoreType.DMA,
            each, each, each, each, each, each, each, each,
            pltpu.SemaphoreType.DMA((ITERS, 4)),
            pltpu.SemaphoreType.DMA((ITERS, 4)),
        ],
        compiler_params=pltpu.CompilerParams(
            collective_id=0, has_side_effects=True, vmem_limit_bytes=56 * 2**20
        ),
    )(
        rows_here, cols_here, tile_counts, rows_here, cols_here,
        right_side, diag_blocks, precond, tile_values[0, 0],
    )
    return pl.pallas_call(
        part_kernel,
        out_shape=(jax.ShapeDtypeStruct((per_dev, width), F32),) * 2,
        in_specs=[vmem],
        out_specs=(vmem, vmem),
    )(both)


def solution(mesh):
    return jax.shard_map(
        per_device,
        mesh=mesh,
        in_specs=(
            P(("row", "col"), None),
            P(("row", "col"), None, None),
            P(("row", "col"), None, None),
            P("row", "col", None, None, None),
            P("row", "col", None),
            P("row", "col", None),
            P("row", "col"),
        ),
        out_specs=(P(("row", "col"), None), P(("row", "col"), None)),
        check_vma=False,
    )
```

```python
import functools

import jax
import jax.numpy as jnp
from jax import lax
from jax.experimental import pallas as pl
from jax.experimental.pallas import tpu as pltpu
from jax.sharding import PartitionSpec as P

ITERS = 3
LANES = 128
MESH = pl.DeviceIdType.MESH
F32 = jnp.float32
BF16 = jnp.bfloat16


def three_parts(value):
    high = value.astype(BF16)
    rest = value - high.astype(F32)
    middle = rest.astype(BF16)
    low = (rest - middle.astype(F32)).astype(BF16)
    return high, middle, low


def apply_blocks(blocks, vec, out, first, last):
    width = blocks.shape[1]
    turned = jnp.transpose(vec)
    for t in range(first, last):
        out[t : t + 1, 0:width] = jnp.sum(blocks[t] * turned[0:width, t : t + 1], axis=0, keepdims=True)


def total(value):
    return jnp.sum(jnp.sum(value, axis=0, keepdims=True), axis=1, keepdims=True)


def kernel(
    n_row, n_col,
    rows_s, cols_s, count_s, rows_v, cols_v, rhs, diag_hbm, prec_hbm, tile_hbm,
    both_out,
    tiles, diag, prec,
    msg, got_row0, got_row1, got_row2, got_col0, got_col1, got_col2, sum_row, sum_col, out_row, out_col,
    picked, backs, col_ends, row_ends, local, stage, turn, dots, dot_col, dot_row,
    x_v, rh_v, z_v, w_v, r_v, s_v, p_v,
    prec_sem, diag_sem, tile_sem,
    msg_col_ssem, msg_row_ssem, got_row_sem, got_col_sem,
    out_row_ssem, out_col_ssem, sum_row_sem, sum_col_sem,
    dot_ssem, dot_rsem,
):
    got_row_of, got_col_of = (got_row0, got_row1, got_row2), (got_col0, got_col1, got_col2)
    per_dev, width = rhs.shape
    slots = tiles.shape[0]
    wide = stage.shape[1]
    my_row = lax.axis_index("row")
    my_col = lax.axis_index("col")

    barrier = pltpu.get_barrier_semaphore()

    side = 4
    my_z, my_y = my_col // side, my_col % side
    my_x, my_core = my_row // 2, my_row % 2
    far = (2, 1, 3, 0)
    col_peers = [
        lax.rem(my_z + dz, side) * side + lax.rem(my_y + dy, side)
        for dz, dy in sorted(
            ((dz, dy) for dz in far for dy in far if dz or dy),
            key=lambda d: -(min(d[0], side - d[0]) + min(d[1], side - d[1])),
        )
    ]
    row_peers = [
        lax.rem(my_x + dx, side) * 2 + lax.rem(my_core + dc, 2)
        for dx in far for dc in (0, 1) if dx or dc
    ]

    for peer in col_peers:
        pl.semaphore_signal(barrier, inc=1, device_id=(my_row, peer), device_id_type=MESH)
    for peer in row_peers:
        pl.semaphore_signal(barrier, inc=1, device_id=(peer, my_col), device_id_type=MESH)

    part = per_dev // 4
    for k in range(4):
        pltpu.make_async_copy(
            prec_hbm.at[pl.ds(k * part, part)], prec.at[pl.ds(k * part, part)], prec_sem.at[k]
        ).start()
    pltpu.make_async_copy(diag_hbm, diag, diag_sem).start()
    pltpu.make_async_copy(tile_hbm, tiles, tile_sem).start()

    def to_cols(source, target, send_sem, recv_sem):
        for peer in col_peers:
            pltpu.make_async_remote_copy(
                src_ref=source(peer), dst_ref=target, send_sem=send_sem, recv_sem=recv_sem,
                device_id=(my_row, peer), device_id_type=MESH,
            ).start()

    def to_rows(source, target, send_sem, recv_sem):
        for peer in row_peers:
            pltpu.make_async_remote_copy(
                src_ref=source(peer), dst_ref=target, send_sem=send_sem, recv_sem=recv_sem,
                device_id=(peer, my_col), device_id_type=MESH,
            ).start()

    def wait_bytes(ref, sem):
        pltpu.make_async_copy(ref, ref, sem).wait()

    full = width // LANES
    rest_lanes = width - full * LANES
    groups = LANES // rest_lanes
    quarter = per_dev // groups
    body = full * per_dev

    def pack(value, target):
        for k in range(full):
            target[k * per_dev : (k + 1) * per_dev, :] = value[:, k * LANES : (k + 1) * LANES]
        ends = value[:, full * LANES :]
        packed = ends[0:quarter, :]
        for a in range(1, groups):
            packed = packed + pltpu.roll(ends, a * rest_lanes, 1)[a * quarter : (a + 1) * quarter, :]
        target[body:, :] = packed

    def spread(packed, target, first):
        for a in range(groups):
            row = first + a * quarter
            target[row : row + quarter, :] = pltpu.roll(packed, LANES - a * rest_lanes, 1) if a else packed

    col_blocks = pl.ds(0, n_col - 1)
    row_blocks = pl.ds(0, n_row - 1)

    count = count_s[0, 0]
    slot_lane = lax.broadcasted_iota(jnp.int32, (1, slots), 1)
    rows_at = jnp.where(slot_lane < count, rows_v[...], -1)
    cols_at = jnp.where(slot_lane < count, cols_v[...], -1)
    rows_at = jnp.concatenate([rows_at, jnp.full((1, LANES - slots), -1, jnp.int32)], axis=1)

    def one_hot(at, n_tiles, a=None):
        if a is None:
            tile = lax.broadcasted_iota(jnp.int32, (n_tiles, at.shape[1]), 0)
        else:
            row = lax.broadcasted_iota(jnp.int32, (n_tiles // groups, at.shape[1]), 0)
            tile = row // quarter * per_dev + a * quarter + row % quarter
        return (tile == at).astype(F32).astype(BF16)

    n_rows, n_cols = n_col * per_dev, n_row * per_dev
    pick_row = jnp.concatenate([one_hot(rows_at, n_rows)] * 3, axis=1)
    pick_row_end = jnp.concatenate([one_hot(rows_at, n_rows, a) for a in range(groups) for _ in range(3)], axis=1)
    pick_col = one_hot(jnp.concatenate([cols_at] * 3, axis=1), n_cols)
    in_group = lax.broadcasted_iota(jnp.int32, (n_cols // groups, groups * slots), 1) // slots
    pick_col_end = jnp.concatenate([one_hot(jnp.concatenate([cols_at] * groups, axis=1), n_cols, in_group)] * 3, axis=1)

    dot_lane = lax.broadcasted_iota(jnp.int32, (8, LANES), 1)
    valid = lax.broadcasted_iota(jnp.int32, (per_dev, wide), 1) < width

    for ref in (local, backs, x_v, rh_v, stage):
        ref[...] = jnp.zeros_like(ref)
    rh_v[:, 0:width] = rhs[...]

    residual = rh_v[...]
    for k in range(4):
        pltpu.make_async_copy(
            prec_hbm.at[pl.ds(k * part, part)], prec.at[pl.ds(k * part, part)], prec_sem.at[k]
        ).wait()
        apply_blocks(prec, residual, stage, k * part, (k + 1) * part)
    pack(stage[...], msg.at[0])

    pl.semaphore_wait(barrier, n_col + n_row - 2)

    def small(j, k, along_row):
        if along_row:
            target, me, send = dot_row.at[j, k], my_col, to_cols
        else:
            target, me, send = dot_col.at[j, k], my_row, to_rows
        send(lambda peer: dots.at[j, k], target.at[me], dot_ssem.at[j, k], dot_rsem.at[j, k])
        target[me] = dots[j, k]

    def small_sum(j, k, along_row):
        source, peers = (dot_row, n_col - 1) if along_row else (dot_col, n_row - 1)
        wait_bytes(source.at[j, k, pl.ds(0, peers)], dot_rsem.at[j, k])
        return jnp.sum(source[j, k], axis=0)

    def in_lanes(*values):
        packed = jnp.zeros((8, LANES), F32)
        for k, value in enumerate(values):
            packed = jnp.where(dot_lane == k, value, packed)
        return packed

    def vector_of(got, ends, index):
        source, tile = lax.div(index, per_dev), lax.rem(index, per_dev)
        lanes = [got[source, pl.ds(k * per_dev + tile, 1), :] for k in range(full)]
        return jnp.concatenate(lanes + [ends[pl.ds(index, 1), :]], axis=1)

    def lanes_of(packed, n):
        return [packed[0:1, k : k + 1] for k in range(n)]

    for j in range(ITERS):
        last = j == ITERS - 1
        got_row, got_col = got_row_of[j], got_col_of[j]
        to_rows(lambda peer: msg.at[j], got_col.at[my_row], msg_row_ssem.at[j], got_col_sem.at[j])
        to_cols(lambda peer: msg.at[j], got_row.at[my_col], msg_col_ssem.at[j], got_row_sem.at[j])
        zh = stage[...]
        rh = rh_v[...]
        got_col[my_row] = msg[j]
        got_row[my_col] = msg[j]

        if j == 0:
            pltpu.make_async_copy(diag_hbm, diag, diag_sem).wait()
        apply_blocks(diag, zh, local, 0, per_dev)
        own = zh * local[...]
        early = [total(own), total(rh * zh)]
        if j > 0:
            z, w, r, s = z_v[...], w_v[...], r_v[...], s_v[...]
            early += [total(rh * z + r * zh), total(zh * w), total(zh * s), total(z * s)]
        dots[j, 0] = in_lanes(*early)
        small(j, 0, True)

        if j == 0:
            pltpu.make_async_copy(tile_hbm, tiles, tile_sem).wait()
        wait_bytes(got_col.at[row_blocks], got_col_sem.at[j])
        for q in range(n_row):
            spread(got_col[q, body:, :], col_ends, q * per_dev)
        turned_lane = lax.broadcasted_iota(jnp.int32, (width, LANES), 1)
        products = jnp.zeros((width, LANES), F32)
        for slot in range(slots):
            index = jnp.clip(cols_s[0, slot], 0, n_cols - 1)
            vector = vector_of(got_col, col_ends, index)[:, 0:width]
            product = jnp.sum(tiles[slot] * vector, axis=1, keepdims=True)
            products = jnp.where(turned_lane == slot, product, products)
        parts = jnp.concatenate(three_parts(products), axis=1)
        across = (((1,), (1,)), ((), ()))
        sums = lax.dot_general(pick_row, parts[0 : full * LANES], across, preferred_element_type=F32)
        for k in range(full):
            out_row[j, :, k * per_dev : (k + 1) * per_dev, :] = sums[:, k * LANES : (k + 1) * LANES].reshape(n_col, per_dev, LANES)
        ends = parts[full * LANES :]
        gap = jnp.zeros_like(ends)
        ends = jnp.concatenate(
            [jnp.concatenate([ends if k == a else gap for k in range(groups)], axis=0) for a in range(groups)], axis=1
        )
        sums = lax.dot_general(pick_row_end, ends, across, preferred_element_type=F32)
        for q in range(n_col):
            out_row[j, q, body:, :] = sums[q * quarter : (q + 1) * quarter, :]

        def send_out_row():
            to_cols(lambda peer: out_row.at[j, peer], sum_row.at[j, my_col], out_row_ssem.at[j], sum_row_sem.at[j])
            sum_row[j, my_col] = out_row[j, my_col]

        if not last:
            send_out_row()

        wait_bytes(got_row.at[col_blocks], got_row_sem.at[j])

        def send_late():
            shared = jnp.sum(out_row[j] * got_row[...], axis=0)
            dots[j, 2] = in_lanes(total(own) + 2.0 * total(shared))
            small(j, 2, last)

        if last:
            send_late()
            send_out_row()
        dots[j, 1] = small_sum(j, 0, True)
        small(j, 1, False)

        for q in range(n_col):
            spread(got_row[q, body:, :], row_ends, q * per_dev)
        for slot in range(slots):
            index = jnp.clip(rows_s[0, slot], 0, n_rows - 1)
            picked[slot : slot + 1, :] = vector_of(got_row, row_ends, index)
        turned = jnp.transpose(picked[...])
        for slot in range(slots):
            backs[slot : slot + 1, 0:width] = jnp.sum(
                tiles[slot] * turned[0:width, slot : slot + 1], axis=0, keepdims=True
            )
        parts = jnp.concatenate(three_parts(backs[:, 0 : full * LANES]), axis=0)
        sums = jnp.dot(pick_col, parts, preferred_element_type=F32)
        for k in range(full):
            out_col[j, :, k * per_dev : (k + 1) * per_dev, :] = sums[:, k * LANES : (k + 1) * LANES].reshape(n_row, per_dev, LANES)
        ends = backs[:, full * LANES :]
        ends = jnp.concatenate([ends] + [pltpu.roll(ends, a * rest_lanes, 1) for a in range(1, groups)], axis=0)
        sums = jnp.dot(pick_col_end, jnp.concatenate(three_parts(ends), axis=0), preferred_element_type=F32)
        for q in range(n_row):
            out_col[j, q, body:, :] = sums[q * quarter : (q + 1) * quarter, :]
        to_rows(lambda peer: out_col.at[j, peer], sum_col.at[j, my_row], out_col_ssem.at[j], sum_col_sem.at[j])
        sum_col[j, my_row] = out_col[j, my_row]

        if not last:
            send_late()
        dots[j, 3] = small_sum(j, 2, last)
        small(j, 3, not last)

        if j == 0:
            curve_h, gamma = lanes_of(small_sum(j, 1, False), 2)
            predicted = gamma / curve_h
            z, r = zh, rh
            p = z
        else:
            curve_h, gamma_h, gamma_x, zh_w, zh_s, z_s = lanes_of(small_sum(j, 1, False), 6)
            delta_h = lanes_of(small_sum(j - 1, 3, True), 1)[0]
            if j == 1:
                delta = curve = delta_h
            else:
                delta = rest * (rest * delta_h + twice) + theta * theta * delta
                curve = delta + beta * (cross + beta * curve)
            alpha = gamma / curve
            theta = (predicted - alpha) / predicted
            rest = 1.0 - theta
            beta = (rest * (rest * gamma_h + theta * gamma_x) + theta * theta * gamma) / gamma
            gamma = beta * gamma
            cross = 2.0 * (rest * zh_s + theta * z_s)
            twice = 2.0 * theta * zh_w
            predicted = gamma_h / curve_h
            x_v[...] = x_v[...] + alpha * p_v[...]
            z = rest * zh + theta * z
            r = rest * rh + theta * r
            p = z + beta * p_v[...]
            kept_w = theta * w
            kept_s = beta * s

        wait_bytes(sum_col.at[j, row_blocks], sum_col_sem.at[j])
        image = jnp.sum(sum_col[j], axis=0)
        wait_bytes(sum_row.at[j, col_blocks], sum_row_sem.at[j])
        image = image + jnp.sum(sum_row[j], axis=0)
        for k in range(full):
            turn[:, k * LANES : (k + 1) * LANES] = image[k * per_dev : (k + 1) * per_dev, :]
        spread(image[body:, :], turn.at[:, pl.ds(full * LANES, LANES)], 0)
        image = local[...] + jnp.where(valid, turn[...], 0.0)
        w = image if j == 0 else rest * image + kept_w
        s = w if j == 0 else w + kept_s
        if not last:
            rh = r - predicted * s
            rh_v[...] = rh
            apply_blocks(prec, rh, stage, 0, per_dev)
            pack(stage[...], msg.at[j + 1])
            z_v[...], w_v[...], r_v[...], s_v[...], p_v[...] = z, w, r, s, p

    delta_h = lanes_of(small_sum(ITERS - 1, 3, False), 1)[0]
    delta = rest * (rest * delta_h + twice) + theta * theta * delta
    alpha = gamma / (delta + beta * (cross + beta * curve))
    x = x_v[...] + alpha * p
    r = r - alpha * s
    both_out[0] = x[:, 0:width]
    both_out[1] = r[:, 0:width]

    for j in range(ITERS):
        wait_bytes(got_col_of[j].at[row_blocks], msg_row_ssem.at[j])
        wait_bytes(got_row_of[j].at[col_blocks], msg_col_ssem.at[j])
        wait_bytes(sum_row.at[j, col_blocks], out_row_ssem.at[j])
        wait_bytes(sum_col.at[j, row_blocks], out_col_ssem.at[j])
        for k in range(4):
            along_row = k == 0 or (k == 2) == (j == ITERS - 1) and k > 1
            source, peers = (dot_row, n_col - 1) if along_row else (dot_col, n_row - 1)
            wait_bytes(source.at[j, k, pl.ds(0, peers)], dot_ssem.at[j, k])


def part_kernel(both, sol_out, res_out):
    sol_out[...] = both[0]
    res_out[...] = both[1]


def per_device(right_side, diag_blocks, precond, tile_values, pair_rows, pair_cols, tile_counts):
    n_row = lax.axis_size("row")
    n_col = lax.axis_size("col")
    per_dev, width = right_side.shape
    slots = tile_values.shape[2]
    wide = -(-width // LANES) * LANES
    rows_here = pair_rows[0]
    cols_here = pair_cols[0]
    smem = pl.BlockSpec(memory_space=pltpu.SMEM)
    vmem = pl.BlockSpec(memory_space=pltpu.VMEM)
    anywhere = pl.BlockSpec(memory_space=pl.ANY)
    vector = pltpu.VMEM((per_dev, wide), F32)
    length = per_dev * width // LANES
    row_area = pltpu.VMEM((ITERS, n_col, length, LANES), F32)
    col_area = pltpu.VMEM((ITERS, n_row, length, LANES), F32)
    got_rows = [pltpu.VMEM((n_col, length, LANES), F32)] * ITERS
    got_cols = [pltpu.VMEM((n_row, length, LANES), F32)] * ITERS
    each = pltpu.SemaphoreType.DMA((ITERS,))
    both = pl.pallas_call(
        functools.partial(kernel, n_row, n_col),
        out_shape=jax.ShapeDtypeStruct((2, per_dev, width), F32),
        in_specs=[smem, smem, smem, vmem, vmem, vmem, anywhere, anywhere, anywhere],
        out_specs=vmem,
        scratch_shapes=[
            pltpu.VMEM((slots, width, width), F32),
            pltpu.VMEM((per_dev, width, width), F32),
            pltpu.VMEM((per_dev, width, width), F32),
            pltpu.VMEM((ITERS, length, LANES), F32),
            *got_rows, *got_cols, row_area, col_area, row_area, col_area,
            pltpu.VMEM((slots, wide), F32),
            pltpu.VMEM((slots, wide), F32),
            pltpu.VMEM((n_row * per_dev, LANES), F32),
            pltpu.VMEM((n_col * per_dev, LANES), F32),
            vector, vector, vector,
            pltpu.VMEM((ITERS, 4, 8, LANES), F32),
            pltpu.VMEM((ITERS, 4, n_row, 8, LANES), F32),
            pltpu.VMEM((ITERS, 4, n_col, 8, LANES), F32),
            vector, vector, vector, vector, vector, vector, vector,
            pltpu.SemaphoreType.DMA((4,)),
            pltpu.SemaphoreType.DMA,
            pltpu.SemaphoreType.DMA,
            each, each, each, each, each, each, each, each,
            pltpu.SemaphoreType.DMA((ITERS, 4)),
            pltpu.SemaphoreType.DMA((ITERS, 4)),
        ],
        compiler_params=pltpu.CompilerParams(
            collective_id=0, has_side_effects=True, vmem_limit_bytes=56 * 2**20
        ),
    )(
        rows_here, cols_here, tile_counts, rows_here, cols_here,
        right_side, diag_blocks, precond, tile_values[0, 0],
    )
    return pl.pallas_call(
        part_kernel,
        out_shape=(jax.ShapeDtypeStruct((per_dev, width), F32),) * 2,
        in_specs=[vmem],
        out_specs=(vmem, vmem),
    )(both)


def solution(mesh):
    return jax.shard_map(
        per_device,
        mesh=mesh,
        in_specs=(
            P(("row", "col"), None),
            P(("row", "col"), None, None),
            P(("row", "col"), None, None),
            P("row", "col", None, None, None),
            P("row", "col", None),
            P("row", "col", None),
            P("row", "col"),
        ),
        out_specs=(P(("row", "col"), None), P(("row", "col"), None)),
        check_vma=False,
    )
```

```python
import functools

import jax
import jax.numpy as jnp
from jax import lax
from jax.experimental import pallas as pl
from jax.experimental.pallas import tpu as pltpu
from jax.sharding import PartitionSpec as P

ITERS = 3
LANES = 128
MESH = pl.DeviceIdType.MESH
F32 = jnp.float32
BF16 = jnp.bfloat16


def three_parts(value):
    high = value.astype(BF16)
    rest = value - high.astype(F32)
    middle = rest.astype(BF16)
    low = (rest - middle.astype(F32)).astype(BF16)
    return high, middle, low


def apply_blocks(blocks, vec, out, first, last):
    width = blocks.shape[1]
    turned = jnp.transpose(vec)
    for t in range(first, last):
        out[t : t + 1, 0:width] = jnp.sum(blocks[t] * turned[0:width, t : t + 1], axis=0, keepdims=True)


def total(value):
    return jnp.sum(jnp.sum(value, axis=0, keepdims=True), axis=1, keepdims=True)


def kernel(
    n_row, n_col,
    rows_hbm, cols_hbm, count_hbm, rhs_hbm, diag_hbm, prec_hbm, tile_hbm,
    both_out,
    rows_s, cols_s, rows_v, cols_v, count_v, rhs,
    tiles, diag, prec,
    msg, got_row0, got_row1, got_row2, got_col0, got_col1, got_col2, sum_row, sum_col, out_row, out_col,
    picked, backs, col_ends, row_ends, local, stage, turn, dots, dot_col, dot_row,
    x_v, rh_v, z_v, w_v, r_v, s_v, p_v,
    small_sem, prec_sem, diag_sem, tile_sem,
    msg_col_ssem, msg_row_ssem, got_row_sem, got_col_sem,
    out_row_ssem, out_col_ssem, sum_row_sem, sum_col_sem,
    dot_ssem, dot_rsem,
):
    got_row_of, got_col_of = (got_row0, got_row1, got_row2), (got_col0, got_col1, got_col2)
    per_dev, width = rhs.shape
    slots = tiles.shape[0]
    wide = stage.shape[1]
    my_row = lax.axis_index("row")
    my_col = lax.axis_index("col")

    barrier = pltpu.get_barrier_semaphore()

    side = 4
    my_z, my_y = my_col // side, my_col % side
    my_x, my_core = my_row // 2, my_row % 2
    far = (2, 1, 3, 0)
    col_peers = [
        lax.rem(my_z + dz, side) * side + lax.rem(my_y + dy, side)
        for dz, dy in sorted(
            ((dz, dy) for dz in far for dy in far if dz or dy),
            key=lambda d: -(min(d[0], side - d[0]) + min(d[1], side - d[1])),
        )
    ]
    row_peers = [
        lax.rem(my_x + dx, side) * 2 + lax.rem(my_core + dc, 2)
        for dx in far for dc in (0, 1) if dx or dc
    ]

    for peer in col_peers:
        pl.semaphore_signal(barrier, inc=1, device_id=(my_row, peer), device_id_type=MESH)
    for peer in row_peers:
        pl.semaphore_signal(barrier, inc=1, device_id=(peer, my_col), device_id_type=MESH)

    small_copies = [
        pltpu.make_async_copy(source, target, small_sem.at[k])
        for k, (source, target) in enumerate((
            (rhs_hbm, rhs), (rows_hbm, rows_v), (cols_hbm, cols_v),
            (count_hbm, count_v), (rows_hbm, rows_s), (cols_hbm, cols_s),
        ))
    ]
    for copy in small_copies:
        copy.start()
    part = per_dev // 4
    for k in range(4):
        pltpu.make_async_copy(
            prec_hbm.at[pl.ds(k * part, part)], prec.at[pl.ds(k * part, part)], prec_sem.at[k]
        ).start()
    pltpu.make_async_copy(diag_hbm, diag, diag_sem).start()
    pltpu.make_async_copy(tile_hbm, tiles, tile_sem).start()

    def to_cols(source, target, send_sem, recv_sem):
        for peer in col_peers:
            pltpu.make_async_remote_copy(
                src_ref=source(peer), dst_ref=target, send_sem=send_sem, recv_sem=recv_sem,
                device_id=(my_row, peer), device_id_type=MESH,
            ).start()

    def to_rows(source, target, send_sem, recv_sem):
        for peer in row_peers:
            pltpu.make_async_remote_copy(
                src_ref=source(peer), dst_ref=target, send_sem=send_sem, recv_sem=recv_sem,
                device_id=(peer, my_col), device_id_type=MESH,
            ).start()

    def wait_bytes(ref, sem):
        pltpu.make_async_copy(ref, ref, sem).wait()

    full = width // LANES
    rest_lanes = width - full * LANES
    groups = LANES // rest_lanes
    quarter = per_dev // groups
    body = full * per_dev

    def pack(value, target):
        for k in range(full):
            target[k * per_dev : (k + 1) * per_dev, :] = value[:, k * LANES : (k + 1) * LANES]
        ends = value[:, full * LANES :]
        packed = ends[0:quarter, :]
        for a in range(1, groups):
            packed = packed + pltpu.roll(ends, a * rest_lanes, 1)[a * quarter : (a + 1) * quarter, :]
        target[body:, :] = packed

    def spread(packed, target, first):
        for a in range(groups):
            row = first + a * quarter
            target[row : row + quarter, :] = pltpu.roll(packed, LANES - a * rest_lanes, 1) if a else packed

    col_blocks = pl.ds(0, n_col - 1)
    row_blocks = pl.ds(0, n_row - 1)

    for copy in small_copies:
        copy.wait()
    count = count_v[...]
    slot_lane = lax.broadcasted_iota(jnp.int32, (1, slots), 1)
    rows_at = jnp.where(slot_lane < count, rows_v[...], -1)
    cols_at = jnp.where(slot_lane < count, cols_v[...], -1)
    rows_at = jnp.concatenate([rows_at, jnp.full((1, LANES - slots), -1, jnp.int32)], axis=1)

    def one_hot(at, n_tiles, a=None):
        if a is None:
            tile = lax.broadcasted_iota(jnp.int32, (n_tiles, at.shape[1]), 0)
        else:
            row = lax.broadcasted_iota(jnp.int32, (n_tiles // groups, at.shape[1]), 0)
            tile = row // quarter * per_dev + a * quarter + row % quarter
        return (tile == at).astype(F32).astype(BF16)

    n_rows, n_cols = n_col * per_dev, n_row * per_dev
    pick_row = jnp.concatenate([one_hot(rows_at, n_rows)] * 3, axis=1)
    pick_row_end = jnp.concatenate([one_hot(rows_at, n_rows, a) for a in range(groups) for _ in range(3)], axis=1)
    pick_col = one_hot(jnp.concatenate([cols_at] * 3, axis=1), n_cols)
    in_group = lax.broadcasted_iota(jnp.int32, (n_cols // groups, groups * slots), 1) // slots
    pick_col_end = jnp.concatenate([one_hot(jnp.concatenate([cols_at] * groups, axis=1), n_cols, in_group)] * 3, axis=1)

    dot_lane = lax.broadcasted_iota(jnp.int32, (8, LANES), 1)
    valid = lax.broadcasted_iota(jnp.int32, (per_dev, wide), 1) < width

    for ref in (local, backs, x_v, rh_v, stage):
        ref[...] = jnp.zeros_like(ref)
    rh_v[:, 0:width] = rhs[...]

    residual = rh_v[...]
    for k in range(4):
        pltpu.make_async_copy(
            prec_hbm.at[pl.ds(k * part, part)], prec.at[pl.ds(k * part, part)], prec_sem.at[k]
        ).wait()
        apply_blocks(prec, residual, stage, k * part, (k + 1) * part)
    pack(stage[...], msg.at[0])

    pl.semaphore_wait(barrier, n_col + n_row - 2)

    def small(j, k, along_row):
        if along_row:
            target, me, send = dot_row.at[j, k], my_col, to_cols
        else:
            target, me, send = dot_col.at[j, k], my_row, to_rows
        send(lambda peer: dots.at[j, k], target.at[me], dot_ssem.at[j, k], dot_rsem.at[j, k])
        target[me] = dots[j, k]

    def small_sum(j, k, along_row):
        source, peers = (dot_row, n_col - 1) if along_row else (dot_col, n_row - 1)
        wait_bytes(source.at[j, k, pl.ds(0, peers)], dot_rsem.at[j, k])
        return jnp.sum(source[j, k], axis=0)

    def in_lanes(*values):
        packed = jnp.zeros((8, LANES), F32)
        for k, value in enumerate(values):
            packed = jnp.where(dot_lane == k, value, packed)
        return packed

    def vector_of(got, ends, index):
        source, tile = lax.div(index, per_dev), lax.rem(index, per_dev)
        lanes = [got[source, pl.ds(k * per_dev + tile, 1), :] for k in range(full)]
        return jnp.concatenate(lanes + [ends[pl.ds(index, 1), :]], axis=1)

    def lanes_of(packed, n):
        return [packed[0:1, k : k + 1] for k in range(n)]

    for j in range(ITERS):
        last = j == ITERS - 1
        got_row, got_col = got_row_of[j], got_col_of[j]
        to_rows(lambda peer: msg.at[j], got_col.at[my_row], msg_row_ssem.at[j], got_col_sem.at[j])
        to_cols(lambda peer: msg.at[j], got_row.at[my_col], msg_col_ssem.at[j], got_row_sem.at[j])
        zh = stage[...]
        rh = rh_v[...]
        got_col[my_row] = msg[j]
        got_row[my_col] = msg[j]

        if j == 0:
            pltpu.make_async_copy(diag_hbm, diag, diag_sem).wait()
        apply_blocks(diag, zh, local, 0, per_dev)
        own = zh * local[...]
        early = [total(own), total(rh * zh)]
        if j > 0:
            z, w, r, s = z_v[...], w_v[...], r_v[...], s_v[...]
            early += [total(rh * z + r * zh), total(zh * w), total(zh * s), total(z * s)]
        dots[j, 0] = in_lanes(*early)
        small(j, 0, True)

        if j == 0:
            pltpu.make_async_copy(tile_hbm, tiles, tile_sem).wait()
        wait_bytes(got_col.at[row_blocks], got_col_sem.at[j])
        for q in range(n_row):
            spread(got_col[q, body:, :], col_ends, q * per_dev)
        turned_lane = lax.broadcasted_iota(jnp.int32, (width, LANES), 1)
        products = jnp.zeros((width, LANES), F32)
        for slot in range(slots):
            index = jnp.clip(cols_s[0, slot], 0, n_cols - 1)
            vector = vector_of(got_col, col_ends, index)[:, 0:width]
            product = jnp.sum(tiles[slot] * vector, axis=1, keepdims=True)
            products = jnp.where(turned_lane == slot, product, products)
        parts = jnp.concatenate(three_parts(products), axis=1)
        across = (((1,), (1,)), ((), ()))
        sums = lax.dot_general(pick_row, parts[0 : full * LANES], across, preferred_element_type=F32)
        for k in range(full):
            out_row[j, :, k * per_dev : (k + 1) * per_dev, :] = sums[:, k * LANES : (k + 1) * LANES].reshape(n_col, per_dev, LANES)
        ends = parts[full * LANES :]
        gap = jnp.zeros_like(ends)
        ends = jnp.concatenate(
            [jnp.concatenate([ends if k == a else gap for k in range(groups)], axis=0) for a in range(groups)], axis=1
        )
        sums = lax.dot_general(pick_row_end, ends, across, preferred_element_type=F32)
        for q in range(n_col):
            out_row[j, q, body:, :] = sums[q * quarter : (q + 1) * quarter, :]

        def send_out_row():
            to_cols(lambda peer: out_row.at[j, peer], sum_row.at[j, my_col], out_row_ssem.at[j], sum_row_sem.at[j])
            sum_row[j, my_col] = out_row[j, my_col]

        if not last:
            send_out_row()

        wait_bytes(got_row.at[col_blocks], got_row_sem.at[j])

        def send_late():
            shared = jnp.sum(out_row[j] * got_row[...], axis=0)
            dots[j, 2] = in_lanes(total(own) + 2.0 * total(shared))
            small(j, 2, last)

        if last:
            send_late()
            send_out_row()
        for q in range(n_col):
            spread(got_row[q, body:, :], row_ends, q * per_dev)
        for slot in range(slots):
            index = jnp.clip(rows_s[0, slot], 0, n_rows - 1)
            picked[slot : slot + 1, :] = vector_of(got_row, row_ends, index)
        turned = jnp.transpose(picked[...])
        for slot in range(slots):
            if slot == slots // 4:
                dots[j, 1] = small_sum(j, 0, True)
                small(j, 1, False)
            backs[slot : slot + 1, 0:width] = jnp.sum(
                tiles[slot] * turned[0:width, slot : slot + 1], axis=0, keepdims=True
            )
        parts = jnp.concatenate(three_parts(backs[:, 0 : full * LANES]), axis=0)
        sums = jnp.dot(pick_col, parts, preferred_element_type=F32)
        for k in range(full):
            out_col[j, :, k * per_dev : (k + 1) * per_dev, :] = sums[:, k * LANES : (k + 1) * LANES].reshape(n_row, per_dev, LANES)
        ends = backs[:, full * LANES :]
        ends = jnp.concatenate([ends] + [pltpu.roll(ends, a * rest_lanes, 1) for a in range(1, groups)], axis=0)
        sums = jnp.dot(pick_col_end, jnp.concatenate(three_parts(ends), axis=0), preferred_element_type=F32)
        for q in range(n_row):
            out_col[j, q, body:, :] = sums[q * quarter : (q + 1) * quarter, :]
        to_rows(lambda peer: out_col.at[j, peer], sum_col.at[j, my_row], out_col_ssem.at[j], sum_col_sem.at[j])
        sum_col[j, my_row] = out_col[j, my_row]

        if not last:
            send_late()
        dots[j, 3] = small_sum(j, 2, last)
        small(j, 3, not last)

        if j == 0:
            curve_h, gamma = lanes_of(small_sum(j, 1, False), 2)
            predicted = gamma / curve_h
            z, r = zh, rh
            p = z
        else:
            curve_h, gamma_h, gamma_x, zh_w, zh_s, z_s = lanes_of(small_sum(j, 1, False), 6)
            delta_h = lanes_of(small_sum(j - 1, 3, True), 1)[0]
            if j == 1:
                delta = curve = delta_h
            else:
                delta = rest * (rest * delta_h + twice) + theta * theta * delta
                curve = delta + beta * (cross + beta * curve)
            alpha = gamma / curve
            theta = (predicted - alpha) / predicted
            rest = 1.0 - theta
            beta = (rest * (rest * gamma_h + theta * gamma_x) + theta * theta * gamma) / gamma
            gamma = beta * gamma
            cross = 2.0 * (rest * zh_s + theta * z_s)
            twice = 2.0 * theta * zh_w
            predicted = gamma_h / curve_h
            x_v[...] = x_v[...] + alpha * p_v[...]
            z = rest * zh + theta * z
            r = rest * rh + theta * r
            p = z + beta * p_v[...]
            kept_w = theta * w
            kept_s = beta * s

        wait_bytes(sum_col.at[j, row_blocks], sum_col_sem.at[j])
        image = jnp.sum(sum_col[j], axis=0)
        wait_bytes(sum_row.at[j, col_blocks], sum_row_sem.at[j])
        image = image + jnp.sum(sum_row[j], axis=0)
        for k in range(full):
            turn[:, k * LANES : (k + 1) * LANES] = image[k * per_dev : (k + 1) * per_dev, :]
        spread(image[body:, :], turn.at[:, pl.ds(full * LANES, LANES)], 0)
        image = local[...] + jnp.where(valid, turn[...], 0.0)
        w = image if j == 0 else rest * image + kept_w
        s = w if j == 0 else w + kept_s
        if not last:
            rh = r - predicted * s
            rh_v[...] = rh
            apply_blocks(prec, rh, stage, 0, per_dev)
            pack(stage[...], msg.at[j + 1])
            z_v[...], w_v[...], r_v[...], s_v[...], p_v[...] = z, w, r, s, p

    delta_h = lanes_of(small_sum(ITERS - 1, 3, False), 1)[0]
    delta = rest * (rest * delta_h + twice) + theta * theta * delta
    alpha = gamma / (delta + beta * (cross + beta * curve))
    x = x_v[...] + alpha * p
    r = r - alpha * s
    both_out[0] = x[:, 0:width]
    both_out[1] = r[:, 0:width]

    for j in range(ITERS):
        wait_bytes(got_col_of[j].at[row_blocks], msg_row_ssem.at[j])
        wait_bytes(got_row_of[j].at[col_blocks], msg_col_ssem.at[j])
        wait_bytes(sum_row.at[j, col_blocks], out_row_ssem.at[j])
        wait_bytes(sum_col.at[j, row_blocks], out_col_ssem.at[j])
        for k in range(4):
            along_row = k == 0 or (k == 2) == (j == ITERS - 1) and k > 1
            source, peers = (dot_row, n_col - 1) if along_row else (dot_col, n_row - 1)
            wait_bytes(source.at[j, k, pl.ds(0, peers)], dot_ssem.at[j, k])


def part_kernel(both, sol_out, res_out):
    sol_out[...] = both[0]
    res_out[...] = both[1]


def per_device(right_side, diag_blocks, precond, tile_values, pair_rows, pair_cols, tile_counts):
    n_row = lax.axis_size("row")
    n_col = lax.axis_size("col")
    per_dev, width = right_side.shape
    slots = tile_values.shape[2]
    wide = -(-width // LANES) * LANES
    rows_here = pair_rows[0]
    cols_here = pair_cols[0]
    vmem = pl.BlockSpec(memory_space=pltpu.VMEM)
    hbm = pl.BlockSpec(memory_space=pltpu.HBM)
    vector = pltpu.VMEM((per_dev, wide), F32)
    length = per_dev * width // LANES
    row_area = pltpu.VMEM((ITERS, n_col, length, LANES), F32)
    col_area = pltpu.VMEM((ITERS, n_row, length, LANES), F32)
    got_rows = [pltpu.VMEM((n_col, length, LANES), F32)] * ITERS
    got_cols = [pltpu.VMEM((n_row, length, LANES), F32)] * ITERS
    each = pltpu.SemaphoreType.DMA((ITERS,))
    both = pl.pallas_call(
        functools.partial(kernel, n_row, n_col),
        out_shape=jax.ShapeDtypeStruct((2, per_dev, width), F32),
        in_specs=[hbm] * 7,
        out_specs=vmem,
        scratch_shapes=[
            pltpu.SMEM((1, slots), jnp.int32),
            pltpu.SMEM((1, slots), jnp.int32),
            pltpu.VMEM((1, slots), jnp.int32),
            pltpu.VMEM((1, slots), jnp.int32),
            pltpu.VMEM((1, 1), jnp.int32),
            pltpu.VMEM((per_dev, width), F32),
            pltpu.VMEM((slots, width, width), F32),
            pltpu.VMEM((per_dev, width, width), F32),
            pltpu.VMEM((per_dev, width, width), F32),
            pltpu.VMEM((ITERS, length, LANES), F32),
            *got_rows, *got_cols, row_area, col_area, row_area, col_area,
            pltpu.VMEM((slots, wide), F32),
            pltpu.VMEM((slots, wide), F32),
            pltpu.VMEM((n_row * per_dev, LANES), F32),
            pltpu.VMEM((n_col * per_dev, LANES), F32),
            vector, vector, vector,
            pltpu.VMEM((ITERS, 4, 8, LANES), F32),
            pltpu.VMEM((ITERS, 4, n_row, 8, LANES), F32),
            pltpu.VMEM((ITERS, 4, n_col, 8, LANES), F32),
            vector, vector, vector, vector, vector, vector, vector,
            pltpu.SemaphoreType.DMA((6,)),
            pltpu.SemaphoreType.DMA((4,)),
            pltpu.SemaphoreType.DMA,
            pltpu.SemaphoreType.DMA,
            each, each, each, each, each, each, each, each,
            pltpu.SemaphoreType.DMA((ITERS, 4)),
            pltpu.SemaphoreType.DMA((ITERS, 4)),
        ],
        compiler_params=pltpu.CompilerParams(
            collective_id=0, has_side_effects=True, vmem_limit_bytes=56 * 2**20
        ),
    )(
        rows_here, cols_here, tile_counts, right_side, diag_blocks, precond, tile_values[0, 0],
    )
    return pl.pallas_call(
        part_kernel,
        out_shape=(jax.ShapeDtypeStruct((per_dev, width), F32),) * 2,
        in_specs=[vmem],
        out_specs=(vmem, vmem),
    )(both)


def solution(mesh):
    return jax.shard_map(
        per_device,
        mesh=mesh,
        in_specs=(
            P(("row", "col"), None),
            P(("row", "col"), None, None),
            P(("row", "col"), None, None),
            P("row", "col", None, None, None),
            P("row", "col", None),
            P("row", "col", None),
            P("row", "col"),
        ),
        out_specs=(P(("row", "col"), None), P(("row", "col"), None)),
        check_vma=False,
    )
```

```python
import functools

import jax
import jax.numpy as jnp
from jax import lax
from jax.experimental import pallas as pl
from jax.experimental.pallas import tpu as pltpu
from jax.sharding import PartitionSpec as P

ITERS = 3
LANES = 128
MESH = pl.DeviceIdType.MESH
F32 = jnp.float32
BF16 = jnp.bfloat16


def three_parts(value):
    high = value.astype(BF16)
    rest = value - high.astype(F32)
    middle = rest.astype(BF16)
    low = (rest - middle.astype(F32)).astype(BF16)
    return high, middle, low


def apply_blocks(blocks, vec, out, first, last):
    width = blocks.shape[1]
    turned = jnp.transpose(vec)
    for t in range(first, last):
        out[t : t + 1, 0:width] = jnp.sum(blocks[t] * turned[0:width, t : t + 1], axis=0, keepdims=True)


def total(value):
    return jnp.sum(jnp.sum(value, axis=0, keepdims=True), axis=1, keepdims=True)


def kernel(
    n_row, n_col,
    rows_hbm, cols_hbm, count_hbm, rhs_hbm, diag_hbm, prec_hbm, tile_hbm,
    both_out,
    rows_s, cols_s, rows_v, cols_v, count_v, rhs,
    tiles, diag, prec,
    msg, got_row0, got_row1, got_row2, got_col0, got_col1, got_col2, sum_row, sum_col, out_row, out_col,
    picked, backs, col_ends, row_ends, local, stage, turn, dots, dot_col, dot_row,
    x_v, rh_v, z_v, w_v, r_v, s_v, p_v,
    small_sem, prec_sem, diag_sem, tile_sem,
    msg_col_ssem, msg_row_ssem, got_row_sem, got_col_sem,
    out_row_ssem, out_col_ssem, sum_row_sem, sum_col_sem,
    dot_ssem, dot_rsem,
):
    got_row_of, got_col_of = (got_row0, got_row1, got_row2), (got_col0, got_col1, got_col2)
    per_dev, width = rhs.shape
    slots = tiles.shape[0]
    wide = stage.shape[1]
    my_row = lax.axis_index("row")
    my_col = lax.axis_index("col")

    barrier = pltpu.get_barrier_semaphore()

    side = 4
    my_z, my_y = my_col // side, my_col % side
    my_x, my_core = my_row // 2, my_row % 2
    far = (2, 1, 3, 0)
    col_peers = [
        lax.rem(my_z + dz, side) * side + lax.rem(my_y + dy, side)
        for dz in far for dy in far if dz or dy
    ]
    row_peers = [
        lax.rem(my_x + dx, side) * 2 + lax.rem(my_core + dc, 2)
        for dx in far for dc in (0, 1) if dx or dc
    ]

    for peer in col_peers:
        pl.semaphore_signal(barrier, inc=1, device_id=(my_row, peer), device_id_type=MESH)
    for peer in row_peers:
        pl.semaphore_signal(barrier, inc=1, device_id=(peer, my_col), device_id_type=MESH)

    small_copies = [
        pltpu.make_async_copy(source, target, small_sem.at[k])
        for k, (source, target) in enumerate((
            (rhs_hbm, rhs), (rows_hbm, rows_v), (cols_hbm, cols_v),
            (count_hbm, count_v), (rows_hbm, rows_s), (cols_hbm, cols_s),
        ))
    ]
    for copy in small_copies:
        copy.start()
    part = per_dev // 4
    for k in range(4):
        pltpu.make_async_copy(
            prec_hbm.at[pl.ds(k * part, part)], prec.at[pl.ds(k * part, part)], prec_sem.at[k]
        ).start()
    pltpu.make_async_copy(diag_hbm, diag, diag_sem).start()
    pltpu.make_async_copy(tile_hbm, tiles, tile_sem).start()

    def to_cols(source, target, send_sem, recv_sem):
        for peer in col_peers:
            pltpu.make_async_remote_copy(
                src_ref=source(peer), dst_ref=target, send_sem=send_sem, recv_sem=recv_sem,
                device_id=(my_row, peer), device_id_type=MESH,
            ).start()

    def to_rows(source, target, send_sem, recv_sem):
        for peer in row_peers:
            pltpu.make_async_remote_copy(
                src_ref=source(peer), dst_ref=target, send_sem=send_sem, recv_sem=recv_sem,
                device_id=(peer, my_col), device_id_type=MESH,
            ).start()

    def wait_bytes(ref, sem):
        pltpu.make_async_copy(ref, ref, sem).wait()

    full = width // LANES
    rest_lanes = width - full * LANES
    groups = LANES // rest_lanes
    quarter = per_dev // groups
    body = full * per_dev

    def pack(value, target):
        for k in range(full):
            target[k * per_dev : (k + 1) * per_dev, :] = value[:, k * LANES : (k + 1) * LANES]
        ends = value[:, full * LANES :]
        packed = ends[0:quarter, :]
        for a in range(1, groups):
            packed = packed + pltpu.roll(ends, a * rest_lanes, 1)[a * quarter : (a + 1) * quarter, :]
        target[body:, :] = packed

    def spread(packed, target, first):
        for a in range(groups):
            row = first + a * quarter
            target[row : row + quarter, :] = pltpu.roll(packed, LANES - a * rest_lanes, 1) if a else packed

    col_blocks = pl.ds(0, n_col - 1)
    row_blocks = pl.ds(0, n_row - 1)

    for copy in small_copies:
        copy.wait()
    count = count_v[...]
    slot_lane = lax.broadcasted_iota(jnp.int32, (1, slots), 1)
    rows_at = jnp.where(slot_lane < count, rows_v[...], -1)
    cols_at = jnp.where(slot_lane < count, cols_v[...], -1)
    rows_at = jnp.concatenate([rows_at, jnp.full((1, LANES - slots), -1, jnp.int32)], axis=1)

    def one_hot(at, n_tiles, a=None):
        if a is None:
            tile = lax.broadcasted_iota(jnp.int32, (n_tiles, at.shape[1]), 0)
        else:
            row = lax.broadcasted_iota(jnp.int32, (n_tiles // groups, at.shape[1]), 0)
            tile = row // quarter * per_dev + a * quarter + row % quarter
        return (tile == at).astype(F32).astype(BF16)

    n_rows, n_cols = n_col * per_dev, n_row * per_dev
    pick_row = jnp.concatenate([one_hot(rows_at, n_rows)] * 3, axis=1)
    pick_row_end = jnp.concatenate([one_hot(rows_at, n_rows, a) for a in range(groups) for _ in range(3)], axis=1)
    pick_col = one_hot(jnp.concatenate([cols_at] * 3, axis=1), n_cols)
    in_group = lax.broadcasted_iota(jnp.int32, (n_cols // groups, groups * slots), 1) // slots
    pick_col_end = jnp.concatenate([one_hot(jnp.concatenate([cols_at] * groups, axis=1), n_cols, in_group)] * 3, axis=1)

    dot_lane = lax.broadcasted_iota(jnp.int32, (8, LANES), 1)
    valid = lax.broadcasted_iota(jnp.int32, (per_dev, wide), 1) < width

    for ref in (local, backs, x_v, rh_v, stage):
        ref[...] = jnp.zeros_like(ref)
    rh_v[:, 0:width] = rhs[...]

    residual = rh_v[...]
    for k in range(4):
        pltpu.make_async_copy(
            prec_hbm.at[pl.ds(k * part, part)], prec.at[pl.ds(k * part, part)], prec_sem.at[k]
        ).wait()
        apply_blocks(prec, residual, stage, k * part, (k + 1) * part)
    pack(stage[...], msg.at[0])

    pl.semaphore_wait(barrier, n_col + n_row - 2)

    def small(j, k, along_row):
        if along_row:
            target, me, send = dot_row.at[j, k], my_col, to_cols
        else:
            target, me, send = dot_col.at[j, k], my_row, to_rows
        send(lambda peer: dots.at[j, k], target.at[me], dot_ssem.at[j, k], dot_rsem.at[j, k])
        target[me] = dots[j, k]

    def small_sum(j, k, along_row):
        source, peers = (dot_row, n_col - 1) if along_row else (dot_col, n_row - 1)
        wait_bytes(source.at[j, k, pl.ds(0, peers)], dot_rsem.at[j, k])
        return jnp.sum(source[j, k], axis=0)

    def in_lanes(*values):
        packed = jnp.zeros((8, LANES), F32)
        for k, value in enumerate(values):
            packed = jnp.where(dot_lane == k, value, packed)
        return packed

    def vector_of(got, ends, index):
        source, tile = lax.div(index, per_dev), lax.rem(index, per_dev)
        lanes = [got[source, pl.ds(k * per_dev + tile, 1), :] for k in range(full)]
        return jnp.concatenate(lanes + [ends[pl.ds(index, 1), :]], axis=1)

    def lanes_of(packed, n):
        return [packed[0:1, k : k + 1] for k in range(n)]

    for j in range(ITERS):
        last = j == ITERS - 1
        got_row, got_col = got_row_of[j], got_col_of[j]
        to_rows(lambda peer: msg.at[j], got_col.at[my_row], msg_row_ssem.at[j], got_col_sem.at[j])
        to_cols(lambda peer: msg.at[j], got_row.at[my_col], msg_col_ssem.at[j], got_row_sem.at[j])
        zh = stage[...]
        rh = rh_v[...]
        got_col[my_row] = msg[j]
        got_row[my_col] = msg[j]

        if j == 0:
            pltpu.make_async_copy(diag_hbm, diag, diag_sem).wait()
        apply_blocks(diag, zh, local, 0, per_dev)
        own = zh * local[...]
        early = [total(own), total(rh * zh)]
        if j > 0:
            z, w, r, s = z_v[...], w_v[...], r_v[...], s_v[...]
            early += [total(rh * z + r * zh), total(zh * w), total(zh * s), total(z * s)]
        dots[j, 0] = in_lanes(*early)
        small(j, 0, True)

        if j == 0:
            pltpu.make_async_copy(tile_hbm, tiles, tile_sem).wait()
        wait_bytes(got_col.at[row_blocks], got_col_sem.at[j])
        for q in range(n_row):
            spread(got_col[q, body:, :], col_ends, q * per_dev)
        turned_lane = lax.broadcasted_iota(jnp.int32, (width, LANES), 1)
        products = jnp.zeros((width, LANES), F32)
        for slot in range(slots):
            index = jnp.clip(cols_s[0, slot], 0, n_cols - 1)
            vector = vector_of(got_col, col_ends, index)[:, 0:width]
            product = jnp.sum(tiles[slot] * vector, axis=1, keepdims=True)
            products = jnp.where(turned_lane == slot, product, products)
        parts = jnp.concatenate(three_parts(products), axis=1)
        across = (((1,), (1,)), ((), ()))
        sums = lax.dot_general(pick_row, parts[0 : full * LANES], across, preferred_element_type=F32)
        for k in range(full):
            out_row[j, :, k * per_dev : (k + 1) * per_dev, :] = sums[:, k * LANES : (k + 1) * LANES].reshape(n_col, per_dev, LANES)
        ends = parts[full * LANES :]
        gap = jnp.zeros_like(ends)
        ends = jnp.concatenate(
            [jnp.concatenate([ends if k == a else gap for k in range(groups)], axis=0) for a in range(groups)], axis=1
        )
        sums = lax.dot_general(pick_row_end, ends, across, preferred_element_type=F32)
        for q in range(n_col):
            out_row[j, q, body:, :] = sums[q * quarter : (q + 1) * quarter, :]

        def send_out_row():
            to_cols(lambda peer: out_row.at[j, peer], sum_row.at[j, my_col], out_row_ssem.at[j], sum_row_sem.at[j])
            sum_row[j, my_col] = out_row[j, my_col]

        send_out_row()

        wait_bytes(got_row.at[col_blocks], got_row_sem.at[j])

        def send_late():
            shared = jnp.sum(out_row[j] * got_row[...], axis=0)
            dots[j, 2] = in_lanes(total(own) + 2.0 * total(shared))
            small(j, 2, False)

        if last:
            send_late()
        for q in range(n_col):
            spread(got_row[q, body:, :], row_ends, q * per_dev)
        for slot in range(slots):
            index = jnp.clip(rows_s[0, slot], 0, n_rows - 1)
            picked[slot : slot + 1, :] = vector_of(got_row, row_ends, index)
        turned = jnp.transpose(picked[...])
        for slot in range(slots):
            if slot == slots // 4:
                dots[j, 1] = small_sum(j, 0, True)
                small(j, 1, False)
            backs[slot : slot + 1, 0:width] = jnp.sum(
                tiles[slot] * turned[0:width, slot : slot + 1], axis=0, keepdims=True
            )
        parts = jnp.concatenate(three_parts(backs[:, 0 : full * LANES]), axis=0)
        sums = jnp.dot(pick_col, parts, preferred_element_type=F32)
        for k in range(full):
            out_col[j, :, k * per_dev : (k + 1) * per_dev, :] = sums[:, k * LANES : (k + 1) * LANES].reshape(n_row, per_dev, LANES)
        ends = backs[:, full * LANES :]
        ends = jnp.concatenate([ends] + [pltpu.roll(ends, a * rest_lanes, 1) for a in range(1, groups)], axis=0)
        sums = jnp.dot(pick_col_end, jnp.concatenate(three_parts(ends), axis=0), preferred_element_type=F32)
        for q in range(n_row):
            out_col[j, q, body:, :] = sums[q * quarter : (q + 1) * quarter, :]
        to_rows(lambda peer: out_col.at[j, peer], sum_col.at[j, my_row], out_col_ssem.at[j], sum_col_sem.at[j])
        sum_col[j, my_row] = out_col[j, my_row]

        if not last:
            send_late()
        dots[j, 3] = small_sum(j, 2, False)
        small(j, 3, True)

        if j == 0:
            curve_h, gamma = lanes_of(small_sum(j, 1, False), 2)
            predicted = gamma / curve_h
            z, r = zh, rh
            p = z
        else:
            curve_h, gamma_h, gamma_x, zh_w, zh_s, z_s = lanes_of(small_sum(j, 1, False), 6)
            delta_h = lanes_of(small_sum(j - 1, 3, True), 1)[0]
            if j == 1:
                delta = curve = delta_h
            else:
                delta = rest * (rest * delta_h + twice) + theta * theta * delta
                curve = delta + beta * (cross + beta * curve)
            alpha = gamma / curve
            theta = (predicted - alpha) / predicted
            rest = 1.0 - theta
            beta = (rest * (rest * gamma_h + theta * gamma_x) + theta * theta * gamma) / gamma
            gamma = beta * gamma
            cross = 2.0 * (rest * zh_s + theta * z_s)
            twice = 2.0 * theta * zh_w
            predicted = gamma_h / curve_h
            x_v[...] = x_v[...] + alpha * p_v[...]
            z = rest * zh + theta * z
            r = rest * rh + theta * r
            p = z + beta * p_v[...]
            kept_w = theta * w
            kept_s = beta * s

        wait_bytes(sum_col.at[j, row_blocks], sum_col_sem.at[j])
        image = jnp.sum(sum_col[j], axis=0)
        wait_bytes(sum_row.at[j, col_blocks], sum_row_sem.at[j])
        image = image + jnp.sum(sum_row[j], axis=0)
        for k in range(full):
            turn[:, k * LANES : (k + 1) * LANES] = image[k * per_dev : (k + 1) * per_dev, :]
        spread(image[body:, :], turn.at[:, pl.ds(full * LANES, LANES)], 0)
        image = local[...] + jnp.where(valid, turn[...], 0.0)
        w = image if j == 0 else rest * image + kept_w
        s = w if j == 0 else w + kept_s
        if not last:
            rh = r - predicted * s
            rh_v[...] = rh
            apply_blocks(prec, rh, stage, 0, per_dev)
            pack(stage[...], msg.at[j + 1])
            z_v[...], w_v[...], r_v[...], s_v[...], p_v[...] = z, w, r, s, p

    delta_h = lanes_of(small_sum(ITERS - 1, 3, True), 1)[0]
    delta = rest * (rest * delta_h + twice) + theta * theta * delta
    alpha = gamma / (delta + beta * (cross + beta * curve))
    x = x_v[...] + alpha * p
    r = r - alpha * s
    both_out[0] = x[:, 0:width]
    both_out[1] = r[:, 0:width]

    for j in range(ITERS):
        wait_bytes(got_col_of[j].at[row_blocks], msg_row_ssem.at[j])
        wait_bytes(got_row_of[j].at[col_blocks], msg_col_ssem.at[j])
        wait_bytes(sum_row.at[j, col_blocks], out_row_ssem.at[j])
        wait_bytes(sum_col.at[j, row_blocks], out_col_ssem.at[j])
        for k in range(4):
            source, peers = (dot_row, n_col - 1) if k in (0, 3) else (dot_col, n_row - 1)
            wait_bytes(source.at[j, k, pl.ds(0, peers)], dot_ssem.at[j, k])


def part_kernel(both, sol_out, res_out):
    sol_out[...] = both[0]
    res_out[...] = both[1]


def per_device(right_side, diag_blocks, precond, tile_values, pair_rows, pair_cols, tile_counts):
    n_row = lax.axis_size("row")
    n_col = lax.axis_size("col")
    per_dev, width = right_side.shape
    slots = tile_values.shape[2]
    wide = -(-width // LANES) * LANES
    rows_here = pair_rows[0]
    cols_here = pair_cols[0]
    vmem = pl.BlockSpec(memory_space=pltpu.VMEM)
    hbm = pl.BlockSpec(memory_space=pltpu.HBM)
    vector = pltpu.VMEM((per_dev, wide), F32)
    length = per_dev * width // LANES
    row_area = pltpu.VMEM((ITERS, n_col, length, LANES), F32)
    col_area = pltpu.VMEM((ITERS, n_row, length, LANES), F32)
    got_rows = [pltpu.VMEM((n_col, length, LANES), F32)] * ITERS
    got_cols = [pltpu.VMEM((n_row, length, LANES), F32)] * ITERS
    each = pltpu.SemaphoreType.DMA((ITERS,))
    both = pl.pallas_call(
        functools.partial(kernel, n_row, n_col),
        out_shape=jax.ShapeDtypeStruct((2, per_dev, width), F32),
        in_specs=[hbm] * 7,
        out_specs=vmem,
        scratch_shapes=[
            pltpu.SMEM((1, slots), jnp.int32),
            pltpu.SMEM((1, slots), jnp.int32),
            pltpu.VMEM((1, slots), jnp.int32),
            pltpu.VMEM((1, slots), jnp.int32),
            pltpu.VMEM((1, 1), jnp.int32),
            pltpu.VMEM((per_dev, width), F32),
            pltpu.VMEM((slots, width, width), F32),
            pltpu.VMEM((per_dev, width, width), F32),
            pltpu.VMEM((per_dev, width, width), F32),
            pltpu.VMEM((ITERS, length, LANES), F32),
            *got_rows, *got_cols, row_area, col_area, row_area, col_area,
            pltpu.VMEM((slots, wide), F32),
            pltpu.VMEM((slots, wide), F32),
            pltpu.VMEM((n_row * per_dev, LANES), F32),
            pltpu.VMEM((n_col * per_dev, LANES), F32),
            vector, vector, vector,
            pltpu.VMEM((ITERS, 4, 8, LANES), F32),
            pltpu.VMEM((ITERS, 4, n_row, 8, LANES), F32),
            pltpu.VMEM((ITERS, 4, n_col, 8, LANES), F32),
            vector, vector, vector, vector, vector, vector, vector,
            pltpu.SemaphoreType.DMA((6,)),
            pltpu.SemaphoreType.DMA((4,)),
            pltpu.SemaphoreType.DMA,
            pltpu.SemaphoreType.DMA,
            each, each, each, each, each, each, each, each,
            pltpu.SemaphoreType.DMA((ITERS, 4)),
            pltpu.SemaphoreType.DMA((ITERS, 4)),
        ],
        compiler_params=pltpu.CompilerParams(
            collective_id=0, has_side_effects=True, vmem_limit_bytes=56 * 2**20
        ),
    )(
        rows_here, cols_here, tile_counts, right_side, diag_blocks, precond, tile_values[0, 0],
    )
    return pl.pallas_call(
        part_kernel,
        out_shape=(jax.ShapeDtypeStruct((per_dev, width), F32),) * 2,
        in_specs=[vmem],
        out_specs=(vmem, vmem),
    )(both)


def solution(mesh):
    return jax.shard_map(
        per_device,
        mesh=mesh,
        in_specs=(
            P(("row", "col"), None),
            P(("row", "col"), None, None),
            P(("row", "col"), None, None),
            P("row", "col", None, None, None),
            P("row", "col", None),
            P("row", "col", None),
            P("row", "col"),
        ),
        out_specs=(P(("row", "col"), None), P(("row", "col"), None)),
        check_vma=False,
    )
```
